768 devices in a mesh: dom: 96 (over y, z), sub: 8 (over x, core).
Axes of the slice: x: 4, y: 8, z: 12, core: 2. Of those that a mesh axis runs over, the one named last changes fastest.
Arguments:
- start: float32 [64, 196608], P(None, ('dom', 'sub'))
- links: int32 [20, 196608], P(None, ('dom', 'sub')), may hold values from 0 to 1791, as said below
- link_weight: float32 [20, 196608], P(None, ('dom', 'sub')), may hold values from 0 to 1, as said below
- pool_slot: int32 [196608], P(('dom', 'sub')), may hold values from -1 to 511, as said below
Outputs:
- eigen_block: float32 [64, 196608], P(None, ('dom', 'sub'))
- ritz_block: float32 [64, 64], replicated
The draws below stay inside these ranges and needn't reach their ends.
Inputs may be any that keep to these rules, and one draw needn't show every extreme that they name: Entries below 256 name a node of the same device; entries from 256 on name a slot of the pool of the group before, the own group or the group after, 512 slots each, and only nodes with a pool slot have such links; links to a group outside the grid do not occur; an entry with zero weight is padding and names 0. `link_weight`: the affinity is symmetric: where node i links to node j with weight w, node j links to node i with weight w; every node has positive weight on its first 14 links; zero marks padding. `pool_slot`: within each partition group every slot 0 to 511 is held by exactly one node; the number of slots a device holds differs from device to device.
All inputs are finite; a program needn't handle non-finite values.
Results may differ from the reference program's by a relative error of at most 0.00005.
Values sent between devices are 32-bit elements; how exact they have to be, the bound alone decides.
A program may use at most 32 MiB of HBM per device.

```python
import jax
import jax.numpy as jnp
from jax import lax

ROWS_DEV = 256
SLOT_DEV = 64
BLOCK = 64
LOCAL_LINKS = 14
GROUP_LINKS = 4
LINKS = 20
SLOTS = 512
N_DOM = 96
N_SUB = 8


def pair_up(ordering):
    swapped = ordering.reshape(-1, 2)[:, ::-1].reshape(-1)
    return jnp.zeros((ordering.shape[0],), jnp.int32).at[ordering].set(swapped.astype(jnp.int32))


def spread_pairs(ordering, values):
    return jnp.zeros((ordering.shape[0],), jnp.float32).at[ordering].set(jnp.repeat(values, 2))


def graph_tables(key, floor_value, power_value):
    groups = N_DOM
    members = N_SUB
    row_count = ROWS_DEV
    slot_count = SLOT_DEV * N_SUB
    devices = groups * members
    node_count = devices * row_count
    keys = jax.random.split(key, 8)

    def shape_weight(values):
        return floor_value + (1.0 - floor_value) * values ** power_value
    local_keys = jax.random.split(keys[0], devices * LOCAL_LINKS)
    local_orders = jax.vmap(lambda k: jax.random.permutation(k, row_count).astype(jnp.int32))(local_keys)
    local_partner = jax.vmap(pair_up)(local_orders)
    local_values = shape_weight(jax.random.uniform(keys[1], (devices * LOCAL_LINKS, row_count // 2)))
    local_weight = jax.vmap(spread_pairs)(local_orders, local_values)
    local_links = local_partner.reshape(devices, LOCAL_LINKS, row_count).transpose(1, 0, 2).reshape(LOCAL_LINKS, node_count)
    local_weight = local_weight.reshape(devices, LOCAL_LINKS, row_count).transpose(1, 0, 2).reshape(LOCAL_LINKS, node_count)
    boost = jax.random.randint(keys[2], (groups, members, 1), 1, 5)
    base_score = jax.random.randint(keys[3], (groups, members, row_count), 0, 1024)
    in_group = jnp.arange(members * row_count, dtype=jnp.int32).reshape(members, row_count)
    score = (base_score * boost * (members * row_count) + in_group).reshape(groups, members * row_count)
    chosen = lax.top_k(score, slot_count)[1].astype(jnp.int32)
    slot_of = jax.vmap(lambda c: jnp.full((members * row_count,), -1, jnp.int32).at[c].set(jnp.arange(slot_count, dtype=jnp.int32)))(chosen)
    valid = slot_of >= 0
    safe_slot = jnp.maximum(slot_of, 0)
    group_ids = jnp.arange(groups, dtype=jnp.int32)
    group_keys = jax.random.split(keys[4], groups * GROUP_LINKS)
    group_orders = jax.vmap(lambda k: jax.random.permutation(k, slot_count).astype(jnp.int32))(group_keys)
    group_partner = jax.vmap(pair_up)(group_orders).reshape(groups, GROUP_LINKS, slot_count)
    group_values = shape_weight(jax.random.uniform(keys[5], (groups * GROUP_LINKS, slot_count // 2)))
    group_weight = jax.vmap(spread_pairs)(group_orders, group_values).reshape(groups, GROUP_LINKS, slot_count)
    column_ids = jnp.arange(GROUP_LINKS, dtype=jnp.int32)
    picked_partner = group_partner[group_ids[:, None, None], column_ids[None, :, None], safe_slot[:, None, :]]
    picked_weight = group_weight[group_ids[:, None, None], column_ids[None, :, None], safe_slot[:, None, :]]
    group_links = jnp.where(valid[:, None, :], row_count + slot_count + picked_partner, 0)
    group_wts = jnp.where(valid[:, None, :], picked_weight, 0.0)
    group_links = group_links.transpose(1, 0, 2).reshape(GROUP_LINKS, node_count)
    group_wts = group_wts.transpose(1, 0, 2).reshape(GROUP_LINKS, node_count)
    cross_keys = jax.random.split(keys[6], groups)
    cross_orders = jax.vmap(lambda k: jax.random.permutation(k, slot_count).astype(jnp.int32))(cross_keys)
    cross_inverse = jax.vmap(lambda o: jnp.zeros((slot_count,), jnp.int32).at[o].set(jnp.arange(slot_count, dtype=jnp.int32)))(cross_orders)
    cross_values = shape_weight(jax.random.uniform(keys[7], (groups, slot_count)))
    has_right = valid & (group_ids[:, None] < groups - 1)
    right_links = jnp.where(has_right, row_count + 2 * slot_count + cross_orders[group_ids[:, None], safe_slot], 0)
    right_wts = jnp.where(has_right, cross_values[group_ids[:, None], safe_slot], 0.0)
    previous = jnp.maximum(group_ids - 1, 0)
    source = cross_inverse[previous[:, None], safe_slot]
    has_left = valid & (group_ids[:, None] > 0)
    left_links = jnp.where(has_left, row_count + source, 0)
    left_wts = jnp.where(has_left, cross_values[previous[:, None], source], 0.0)
    all_links = jnp.concatenate([local_links, group_links, right_links.reshape(1, node_count), left_links.reshape(1, node_count)], axis=0).astype(jnp.int32)
    all_weights = jnp.concatenate([local_weight, group_wts, right_wts.reshape(1, node_count), left_wts.reshape(1, node_count)], axis=0).astype(jnp.float32)
    return (all_links, all_weights, slot_of.reshape(node_count).astype(jnp.int32))


def draw_start(key, part):
    key = jax.random.fold_in(key, 11)
    first, second = jax.random.split(key, 2)
    node_count = ROWS_DEV * N_DOM * N_SUB
    position = jnp.arange(node_count, dtype=jnp.float32) / node_count
    spread = jnp.exp(jnp.log(10.0) * jax.random.uniform(second, (node_count,))) * 3.0 ** position
    values = jnp.clip(jax.random.normal(first, (BLOCK, node_count)), -5.0, 5.0)
    return (values * spread).astype(jnp.float32)


def draw_links(key, part):
    tables = graph_tables(key, 0.1, 1.0)
    return tables[0]


def draw_link_weight(key, part):
    tables = graph_tables(key, 0.1, 1.0)
    return tables[1]


def draw_pool_slot(key, part):
    tables = graph_tables(key, 0.1, 1.0)
    return tables[2]


def setup_inputs(seed: int = 0) -> dict:
    splits = jax.random.split(jax.random.key(seed), 5)
    return {
        "start": draw_start(jax.random.fold_in(splits[4], 71), 0),
        "links": draw_links(jax.random.fold_in(splits[4], 71), 0),
        "link_weight": draw_link_weight(jax.random.fold_in(splits[4], 71), 0),
        "pool_slot": draw_pool_slot(jax.random.fold_in(splits[4], 71), 0),
    }


def products(left_side, right_side):
    return jnp.dot(left_side, right_side.T, precision=lax.Precision.HIGHEST)

def reduce_basis(gram_sum, mixed_sum, block_size):
    highest = lax.Precision.HIGHEST
    basis_size = gram_sum.shape[0]
    lower_fac = jnp.linalg.cholesky(gram_sum)
    symmetric = 0.5 * (mixed_sum + mixed_sum.T)
    halfway = lax.linalg.triangular_solve(lower_fac, symmetric, left_side=True, lower=True)
    reduced = lax.linalg.triangular_solve(lower_fac, halfway.T, left_side=True, lower=True)
    shifted = 0.5 * (reduced + jnp.eye(basis_size, dtype=jnp.float32))
    filtered = jnp.dot(shifted, shifted, precision=highest)
    filtered = jnp.dot(filtered, filtered, precision=highest)
    start_coords = lower_fac.T[:, :block_size]
    tilted = jnp.dot(filtered, start_coords, precision=highest)
    factor = jnp.linalg.cholesky(jnp.dot(tilted.T, tilted, precision=highest))
    orthonormal = lax.linalg.triangular_solve(factor, tilted.T, left_side=True, lower=True).T
    coeffs = lax.linalg.triangular_solve(lower_fac, orthonormal, left_side=True, lower=True, transpose_a=True)
    ritz_part = jnp.dot(orthonormal.T, jnp.dot(reduced, orthonormal, precision=highest), precision=highest)
    return (coeffs, ritz_part)

def reference(start, links, link_weight, pool_slot):
    highest = lax.Precision.HIGHEST
    block_size = start.shape[0]
    node_count = start.shape[1]
    node_ids = jnp.arange(node_count, dtype=jnp.int32)
    group_ids = (node_ids // (ROWS_DEV * N_SUB)).astype(jnp.int32)
    device_base = (node_ids // ROWS_DEV * ROWS_DEV).astype(jnp.int32)
    area_index = ((links - ROWS_DEV) // SLOTS).astype(jnp.int32)
    slot_index = ((links - ROWS_DEV) % SLOTS).astype(jnp.int32)
    global_index = jnp.where(links < ROWS_DEV, device_base[None, :] + links, node_count + (group_ids[None, :] + area_index) * SLOTS + slot_index).astype(jnp.int32)
    pool_target = jnp.where(pool_slot >= 0, group_ids * SLOTS + pool_slot, N_DOM * SLOTS).astype(jnp.int32)
    degree = lax.optimization_barrier(jnp.sum(link_weight, axis=0))
    root = lax.rsqrt(degree)

    def affinity(vectors):
        scaled = root * vectors
        pools = jnp.zeros((vectors.shape[0], N_DOM * SLOTS + 1), jnp.float32).at[:, pool_target].add(scaled)
        border = jnp.zeros((vectors.shape[0], SLOTS), jnp.float32)
        lookup = jnp.concatenate([scaled, border, pools[:, :N_DOM * SLOTS], border], axis=1)
        summed = jnp.zeros_like(vectors)
        for column in range(LINKS):
            summed = summed + link_weight[column] * jnp.take(lookup, global_index[column], axis=1)
        return root * summed

    def ritz_step(basis, images):
        gram_sum = products(basis, basis) / node_count
        mixed_sum = products(basis, images) / node_count
        return reduce_basis(gram_sum, mixed_sum, block_size)
    image_x = affinity(start)
    image_w = affinity(image_x)
    basis_one = jnp.concatenate([start, image_x], axis=0)
    images_one = jnp.concatenate([image_x, image_w], axis=0)
    coeffs_one, theta_one = ritz_step(basis_one, images_one)
    current = jnp.dot(coeffs_one.T, basis_one, precision=highest)
    current_img = jnp.dot(coeffs_one.T, images_one, precision=highest)
    tail_coef = coeffs_one[block_size:]
    search = jnp.dot(tail_coef.T, image_x, precision=highest)
    search_img = jnp.dot(tail_coef.T, image_w, precision=highest)
    residual = current_img - jnp.dot(theta_one.T, current, precision=highest)
    residual_img = affinity(residual)
    basis_two = jnp.concatenate([current, residual, search], axis=0)
    images_two = jnp.concatenate([current_img, residual_img, search_img], axis=0)
    coeffs_two, ritz_block = ritz_step(basis_two, images_two)
    eigen_block = jnp.dot(coeffs_two.T, basis_two, precision=highest)
    return (eigen_block, ritz_block)
```

```python
import functools

import jax
import jax.numpy as jnp
from jax import lax
from jax.experimental import pallas as pl
from jax.experimental.pallas import tpu as pltpu
from jax.sharding import PartitionSpec as P

MESH = pl.DeviceIdType.MESH
VMEM = pltpu.VMEM
DMA = pltpu.SemaphoreType.DMA
SLOT_DEV = 64
ROUNDS = 3
BUILD_ROWS = 64
N_Z = 12


def split(values):
    high = values.astype(jnp.bfloat16)
    low = (values - high.astype(jnp.float32)).astype(jnp.bfloat16)
    return high, low


def outer(left, right):
    return lax.dot_general(
        left,
        right,
        (((1,), (1,)), ((), ())),
        precision=lax.Precision.HIGHEST,
        preferred_element_type=jnp.float32,
    )


def each(low, high, body):
    lax.fori_loop(low, high, lambda k, c: (body(k), c)[1], 0)


def sums_kernel(
    n_dom,
    n_sub,
    start_ref,
    links_ref,
    weight_ref,
    slot_ref,
    one_ref,
    two_ref,
    sums_ref,
    root_ref,
    place_ref,
    table_hi,
    table_lo,
    contrib,
    gathered,
    pools,
    partial,
    part_in,
    z_in,
    y_in,
    rs_send,
    rs_recv,
    ag_send,
    ag_recv,
    part_send,
    part_recv,
    z_send,
    z_recv,
    y_send,
    y_recv,
    out_send,
    out_recv,
):
    dom = lax.axis_index("dom")
    sub = lax.axis_index("sub")
    n_y = n_dom // N_Z
    row = dom // N_Z
    col = dom % N_Z
    block = start_ref.shape[0]
    nodes = start_ref.shape[1]
    slots = place_ref.shape[0]
    share = block // n_sub
    part = partial.shape[0] // n_sub

    def sub_peer(k):
        return (sub + k) % n_sub

    def dom_peer(area):
        return (dom + area + n_dom - 1) % n_dom

    def z_peer(k):
        return (col + k) % N_Z

    def y_peer(k):
        return (row + k) % n_y

    def remote(src, dst, send, recv, d, s):
        return pltpu.make_async_remote_copy(
            src_ref=src, dst_ref=dst, send_sem=send, recv_sem=recv,
            device_id=(d, s), device_id_type=MESH,
        )

    barrier = pltpu.get_barrier_semaphore()

    def greet(d, s):
        pl.semaphore_signal(barrier, inc=1, device_id=(d, s), device_id_type=MESH)

    each(1, n_sub, lambda k: greet(dom, sub_peer(k)))
    each(0, n_sub, lambda k: greet(dom_peer(0), k))
    each(0, n_sub, lambda k: greet(dom_peer(2), k))
    each(1, N_Z, lambda k: greet(row * N_Z + z_peer(k), sub))
    each(1, n_y, lambda k: greet(y_peer(k) * N_Z + col, sub))

    def rs_copy(j, peer, at):
        return remote(contrib.at[j, peer], gathered.at[j, at],
                      rs_send.at[j, peer], rs_recv.at[j, at], dom, peer)

    def ag_copy(j, to, peer, area, at):
        return remote(pools.at[j, 1, sub], pools.at[j, area, at],
                      ag_send.at[j, to, peer], ag_recv.at[j, area, at], dom_peer(to), peer)

    def rows_of(p):
        return pl.ds(pl.multiple_of(p * part, part), part)

    def part_copy(peer, at):
        return remote(partial.at[rows_of(peer)], part_in.at[at],
                      part_send.at[peer], part_recv.at[at], dom, peer)

    def z_copy(peer, at):
        return remote(z_in.at[col], z_in.at[at],
                      z_send.at[peer], z_recv.at[at], row * N_Z + peer, sub)

    def y_copy(peer, at):
        return remote(y_in.at[row], y_in.at[at],
                      y_send.at[peer], y_recv.at[at], peer * N_Z + col, sub)

    def out_copy(peer, at):
        return remote(sums_ref.at[rows_of(sub)], sums_ref.at[rows_of(at)],
                      out_send.at[peer], out_recv.at[at], dom, peer)

    def total(ref, count):
        result = ref[0]
        for k in range(1, count):
            result = result + ref[k]
        return result

    root_ref[...] = lax.rsqrt(jnp.sum(weight_ref[...], axis=0, keepdims=True))

    def place(i, carry):
        base = pl.multiple_of(i * BUILD_ROWS, BUILD_ROWS)
        ids = base + lax.broadcasted_iota(jnp.int32, (BUILD_ROWS, nodes), 0)
        place_ref[pl.ds(base, BUILD_ROWS), :] = jnp.where(
            ids == slot_ref[...], 1.0, 0.0
        ).astype(jnp.bfloat16)
        return carry

    lax.fori_loop(0, slots // BUILD_ROWS, place, 0)

    def build(i, carry):
        base = pl.multiple_of(i * BUILD_ROWS, BUILD_ROWS)
        ids = base + lax.broadcasted_iota(jnp.int32, (BUILD_ROWS, nodes), 0)
        summed = jnp.zeros((BUILD_ROWS, nodes), jnp.float32)
        for k in range(links_ref.shape[0]):
            summed = summed + jnp.where(
                ids == links_ref[k : k + 1, :], weight_ref[k : k + 1, :], 0.0
            )
        high, low = split(summed * root_ref[...])
        table_hi[pl.ds(base, BUILD_ROWS), :] = high
        table_lo[pl.ds(base, BUILD_ROWS), :] = low
        return carry

    def contribute(j, vectors):
        high, low = split(root_ref[...] * vectors)
        spread = lax.dot_general(
            jnp.concatenate([high, low], axis=0),
            place_ref[...],
            (((1,), (1,)), ((), ())),
            preferred_element_type=jnp.float32,
        )
        contrib[j] = (spread[:block] + spread[block:]).reshape(n_sub, share, slots)
        return high, low

    def apply(high, low, first, count):
        upper = jnp.dot(
            jnp.concatenate([high, low], axis=0),
            table_hi[first : first + count, :],
            preferred_element_type=jnp.float32,
        )
        lower = jnp.dot(
            high, table_lo[first : first + count, :], preferred_element_type=jnp.float32
        )
        return upper[:block] + upper[block:] + lower

    def affinity(j, vectors, meanwhile):
        high, low = contribute(j, vectors)
        if j == 0:
            pl.semaphore_wait(barrier, 3 * n_sub - 1 + N_Z - 1 + n_y - 1)
        each(1, n_sub, lambda k: rs_copy(j, sub_peer(k), sub).start())
        if j == 0:
            lax.fori_loop(0, table_hi.shape[0] // BUILD_ROWS, build, 0)
        gathered[j, sub] = contrib[j, sub]
        summed = apply(high, low, 0, nodes)
        each(1, n_sub, lambda k: rs_copy(j, sub_peer(k), sub_peer(k)).wait_recv())
        pools[j, 1, sub] = total(gathered.at[j], n_sub)
        each(1, n_sub, lambda k: ag_copy(j, 1, sub_peer(k), 1, sub).start())
        each(0, n_sub, lambda k: ag_copy(j, 0, k, 2, sub).start())
        each(0, n_sub, lambda k: ag_copy(j, 2, k, 0, sub).start())
        meanwhile()
        each(1, n_sub, lambda k: ag_copy(j, 1, sub_peer(k), 1, sub_peer(k)).wait_recv())
        for area in (1, 0, 2):
            if area != 1:
                each(0, n_sub, lambda k: ag_copy(j, area, k, area, k).wait_recv())
            high, low = split(pools[j, area].reshape(block, slots))
            summed = summed + apply(high, low, nodes + area * slots, slots)
        return summed

    def moments_zero():
        partial[0:block, 0:block] = outer(start_ref[...], start_ref[...])

    def moments_one():
        partial[0:block, block : 2 * block] = outer(start_ref[...], one_ref[...])
        partial[block : 2 * block, 0:block] = outer(one_ref[...], one_ref[...])

    def moments_two():
        partial[block : 2 * block, block : 2 * block] = outer(one_ref[...], two_ref[...])
        partial[2 * block : 3 * block, 0:block] = outer(two_ref[...], two_ref[...])

    one_ref[...] = affinity(0, start_ref[...], moments_zero)
    two_ref[...] = affinity(1, one_ref[...], moments_one)
    three = affinity(2, two_ref[...], moments_two)
    partial[2 * block : 3 * block, block : 2 * block] = outer(two_ref[...], three)

    each(1, n_sub, lambda k: part_copy(sub_peer(k), sub).start())
    part_in[sub] = partial[rows_of(sub), :]
    each(1, n_sub, lambda k: part_copy(sub_peer(k), sub_peer(k)).wait_recv())
    z_in[col] = total(part_in, n_sub)
    each(1, N_Z, lambda k: z_copy(z_peer(k), col).start())
    each(1, N_Z, lambda k: z_copy(z_peer(k), z_peer(k)).wait_recv())
    y_in[row] = total(z_in, N_Z)
    each(1, n_y, lambda k: y_copy(y_peer(k), row).start())
    each(1, n_y, lambda k: y_copy(y_peer(k), y_peer(k)).wait_recv())
    sums_ref[rows_of(sub), :] = total(y_in, n_y)
    each(1, n_sub, lambda k: out_copy(sub_peer(k), sub).start())
    each(1, n_sub, lambda k: out_copy(sub_peer(k), sub_peer(k)).wait_recv())

    for j in range(ROUNDS):
        each(1, n_sub, lambda k: rs_copy(j, sub_peer(k), sub).wait_send())
        each(1, n_sub, lambda k: ag_copy(j, 1, sub_peer(k), 1, sub).wait_send())
        each(0, n_sub, lambda k: ag_copy(j, 0, k, 2, sub).wait_send())
        each(0, n_sub, lambda k: ag_copy(j, 2, k, 0, sub).wait_send())
    each(1, n_sub, lambda k: part_copy(sub_peer(k), sub).wait_send())
    each(1, N_Z, lambda k: z_copy(z_peer(k), col).wait_send())
    each(1, n_y, lambda k: y_copy(y_peer(k), row).wait_send())
    each(1, n_sub, lambda k: out_copy(sub_peer(k), sub).wait_send())


def powers_and_sums(start, links, link_weight, pool_slot):
    n_dom = lax.axis_size("dom")
    n_sub = lax.axis_size("sub")
    n_y = n_dom // N_Z
    block, nodes = start.shape
    slots = SLOT_DEV * n_sub
    share = block // n_sub
    part = 3 * block // n_sub
    entries = nodes + 3 * slots
    vectors = jax.ShapeDtypeStruct((block, nodes), jnp.float32)
    f32 = jnp.float32
    return pl.pallas_call(
        functools.partial(sums_kernel, n_dom, n_sub),
        out_shape=(vectors, vectors, jax.ShapeDtypeStruct((3 * block, 2 * block), f32)),
        in_specs=[pl.BlockSpec(memory_space=VMEM)] * 4,
        out_specs=(pl.BlockSpec(memory_space=VMEM),) * 3,
        scratch_shapes=[
            VMEM((1, nodes), f32),
            VMEM((slots, nodes), jnp.bfloat16),
            VMEM((entries, nodes), jnp.bfloat16),
            VMEM((entries, nodes), jnp.bfloat16),
            VMEM((ROUNDS, n_sub, share, slots), f32),
            VMEM((ROUNDS, n_sub, share, slots), f32),
            VMEM((ROUNDS, 3, n_sub, share, slots), f32),
            VMEM((3 * block, 2 * block), f32),
            VMEM((n_sub, part, 2 * block), f32),
            VMEM((N_Z, part, 2 * block), f32),
            VMEM((n_y, part, 2 * block), f32),
            DMA((ROUNDS, n_sub)),
            DMA((ROUNDS, n_sub)),
            DMA((ROUNDS, 3, n_sub)),
            DMA((ROUNDS, 3, n_sub)),
            DMA((n_sub,)),
            DMA((n_sub,)),
            DMA((N_Z,)),
            DMA((N_Z,)),
            DMA((n_y,)),
            DMA((n_y,)),
            DMA((n_sub,)),
            DMA((n_sub,)),
        ],
        compiler_params=pltpu.CompilerParams(
            collective_id=0, has_side_effects=True, vmem_limit_bytes=32 * 1024 * 1024
        ),
        name="powers_and_sums",
    )(start, links, link_weight, pool_slot.reshape(1, nodes))


def reduce_basis(gram_sum, mixed_sum, block_size):
    highest = lax.Precision.HIGHEST
    basis_size = gram_sum.shape[0]
    lower_fac = jnp.linalg.cholesky(gram_sum)
    symmetric = 0.5 * (mixed_sum + mixed_sum.T)
    halfway = lax.linalg.triangular_solve(lower_fac, symmetric, left_side=True, lower=True)
    reduced = lax.linalg.triangular_solve(lower_fac, halfway.T, left_side=True, lower=True)
    shifted = 0.5 * (reduced + jnp.eye(basis_size, dtype=jnp.float32))
    filtered = jnp.dot(shifted, shifted, precision=highest)
    filtered = jnp.dot(filtered, filtered, precision=highest)
    start_coords = lower_fac.T[:, :block_size]
    tilted = jnp.dot(filtered, start_coords, precision=highest)
    factor = jnp.linalg.cholesky(jnp.dot(tilted.T, tilted, precision=highest))
    orthonormal = lax.linalg.triangular_solve(factor, tilted.T, left_side=True, lower=True).T
    coeffs = lax.linalg.triangular_solve(
        lower_fac, orthonormal, left_side=True, lower=True, transpose_a=True
    )
    ritz_part = jnp.dot(
        orthonormal.T, jnp.dot(reduced, orthonormal, precision=highest), precision=highest
    )
    return (coeffs, ritz_part)


def per_device(start, links, link_weight, pool_slot):
    highest = lax.Precision.HIGHEST
    block, nodes = start.shape
    node_count = nodes * lax.axis_size("dom") * lax.axis_size("sub")
    one, two, sums = powers_and_sums(start, links, link_weight, pool_slot)
    sums = sums / node_count
    moments = [
        sums[r * block : (r + 1) * block, c * block : (c + 1) * block]
        for r in range(3)
        for c in range(2)
    ]
    moments = [0.5 * (m + m.T) for m in moments]

    def hankel(first, size):
        return jnp.concatenate(
            [
                jnp.concatenate([moments[first + i + j] for j in range(size)], axis=1)
                for i in range(size)
            ],
            axis=0,
        )

    coeffs_one, theta_one = reduce_basis(hankel(0, 2), hankel(1, 2), block)
    head, tail = coeffs_one[:block], coeffs_one[block:]
    nothing = jnp.zeros_like(head)
    residual = jnp.concatenate([nothing, head, tail], axis=0) - jnp.dot(
        jnp.concatenate([head, tail, nothing], axis=0), theta_one, precision=highest
    )
    basis_two = jnp.concatenate(
        [
            jnp.concatenate([head, tail, nothing], axis=0),
            residual,
            jnp.concatenate([nothing, tail, nothing], axis=0),
        ],
        axis=1,
    )

    def project(moment_matrix):
        right = jnp.dot(moment_matrix, basis_two, precision=highest)
        return jnp.dot(basis_two.T, right, precision=highest)

    coeffs_two, ritz_block = reduce_basis(project(hankel(0, 3)), project(hankel(1, 3)), block)
    weights = jnp.dot(basis_two, coeffs_two, precision=highest)
    eigen_block = jnp.dot(
        weights.T, jnp.concatenate([start, one, two], axis=0), precision=highest
    )
    return (eigen_block, ritz_block)


def solution(mesh):
    placed = (
        P(None, ("dom", "sub")),
        P(None, ("dom", "sub")),
        P(None, ("dom", "sub")),
        P(("dom", "sub")),
    )
    return jax.shard_map(
        per_device,
        mesh=mesh,
        in_specs=placed,
        out_specs=(P(None, ("dom", "sub")), P()),
        check_vma=False,
    )
```

```python
import functools

import jax
import jax.numpy as jnp
from jax import lax
from jax.experimental import pallas as pl
from jax.experimental.pallas import tpu as pltpu
from jax.sharding import PartitionSpec as P

MESH = pl.DeviceIdType.MESH
VMEM = pltpu.VMEM
DMA = pltpu.SemaphoreType.DMA
SLOT_DEV = 64
ROUNDS = 3
BUILD_ROWS = 64
N_Z = 12
SUBLANES = 8


def split(values):
    high = values.astype(jnp.bfloat16)
    low = (values - high.astype(jnp.float32)).astype(jnp.bfloat16)
    return high, low


def outer(left, right):
    return lax.dot_general(
        left,
        right,
        (((1,), (1,)), ((), ())),
        precision=lax.Precision.HIGHEST,
        preferred_element_type=jnp.float32,
    )


def each(low, high, body):
    lax.fori_loop(low, high, lambda k, c: (body(k), c)[1], 0)


def sums_kernel(
    n_dom,
    n_sub,
    start_ref,
    links_ref,
    weight_ref,
    slot_ref,
    one_ref,
    two_ref,
    sums_ref,
    root_ref,
    place_ref,
    table_hi,
    table_lo,
    contrib,
    gathered,
    pools,
    partial,
    part_in,
    z_in,
    y_in,
    rs_send,
    rs_recv,
    ag_send,
    ag_recv,
    part_send,
    part_recv,
    z_send,
    z_recv,
    y_send,
    y_recv,
    out_send,
    out_recv,
):
    dom = lax.axis_index("dom")
    sub = lax.axis_index("sub")
    n_y = n_dom // N_Z
    row = dom // N_Z
    col = dom % N_Z
    block = start_ref.shape[0]
    nodes = start_ref.shape[1]
    slots = place_ref.shape[0]
    share = block // n_sub
    part = partial.shape[0] // n_sub

    def sub_peer(k):
        return (sub + k) % n_sub

    def dom_peer(area):
        return (dom + area + n_dom - 1) % n_dom

    def z_peer(k):
        return (col + k) % N_Z

    def y_peer(k):
        return (row + k) % n_y

    def remote(src, dst, send, recv, d, s):
        return pltpu.make_async_remote_copy(
            src_ref=src, dst_ref=dst, send_sem=send, recv_sem=recv,
            device_id=(d, s), device_id_type=MESH,
        )

    barrier = pltpu.get_barrier_semaphore()

    def greet(d, s):
        pl.semaphore_signal(barrier, inc=1, device_id=(d, s), device_id_type=MESH)

    each(1, n_sub, lambda k: greet(dom, sub_peer(k)))
    each(0, n_sub, lambda k: greet(dom_peer(0), k))
    each(0, n_sub, lambda k: greet(dom_peer(2), k))
    each(1, N_Z, lambda k: greet(row * N_Z + z_peer(k), sub))
    each(1, n_y, lambda k: greet(y_peer(k) * N_Z + col, sub))

    def rs_copy(j, peer, at):
        return remote(contrib.at[j, peer], gathered.at[j, at],
                      rs_send.at[j, peer], rs_recv.at[j, at], dom, peer)

    def ag_copy(j, to, peer, area, at):
        return remote(pools.at[j, 1, sub], pools.at[j, area, at],
                      ag_send.at[j, to, peer], ag_recv.at[j, area, at], dom_peer(to), peer)

    def rows_of(p):
        return pl.ds(pl.multiple_of(p * part, part), part)

    def part_copy(peer, at):
        return remote(partial.at[rows_of(peer)], part_in.at[at],
                      part_send.at[peer], part_recv.at[at], dom, peer)

    def z_copy(peer, at):
        return remote(z_in.at[col], z_in.at[at],
                      z_send.at[peer], z_recv.at[at], row * N_Z + peer, sub)

    def y_copy(peer, at):
        return remote(y_in.at[row], y_in.at[at],
                      y_send.at[peer], y_recv.at[at], peer * N_Z + col, sub)

    def out_copy(peer, at):
        return remote(sums_ref.at[rows_of(sub)], sums_ref.at[rows_of(at)],
                      out_send.at[peer], out_recv.at[at], dom, peer)

    def total(ref, count):
        result = ref[0]
        for k in range(1, count):
            result = result + ref[k]
        return result

    root_ref[...] = lax.rsqrt(jnp.sum(weight_ref[...], axis=0, keepdims=True))

    def place(i, carry):
        base = pl.multiple_of(i * BUILD_ROWS, BUILD_ROWS)
        ids = base + lax.broadcasted_iota(jnp.int32, (BUILD_ROWS, nodes), 0)
        place_ref[pl.ds(base, BUILD_ROWS), :] = jnp.where(
            ids == slot_ref[...], 1.0, 0.0
        ).astype(jnp.bfloat16)
        return carry

    lax.fori_loop(0, slots // BUILD_ROWS, place, 0)

    def build(i, carry):
        base = pl.multiple_of(i * BUILD_ROWS, BUILD_ROWS)
        ids = base + lax.broadcasted_iota(jnp.int32, (BUILD_ROWS, nodes), 0)
        summed = jnp.zeros((BUILD_ROWS, nodes), jnp.float32)
        for k in range(links_ref.shape[0]):
            summed = summed + jnp.where(
                ids == links_ref[k : k + 1, :], weight_ref[k : k + 1, :], 0.0
            )
        high, low = split(summed * root_ref[...])
        table_hi[pl.ds(base, BUILD_ROWS), :] = high
        table_lo[pl.ds(base, BUILD_ROWS), :] = low
        return carry

    def contribute(j, vectors):
        high, low = split(root_ref[...] * vectors)
        spread = lax.dot_general(
            jnp.concatenate([high, low], axis=0),
            place_ref[...],
            (((1,), (1,)), ((), ())),
            preferred_element_type=jnp.float32,
        )
        contrib[j] = (spread[:block] + spread[block:]).reshape(n_sub, share, slots)
        return high, low

    def apply(high, low, first, count):
        upper = jnp.dot(
            jnp.concatenate([high, low], axis=0),
            table_hi[first : first + count, :],
            preferred_element_type=jnp.float32,
        )
        lower = jnp.dot(
            high, table_lo[first : first + count, :], preferred_element_type=jnp.float32
        )
        return upper[:block] + upper[block:] + lower

    def affinity(j, vectors, meanwhile):
        high, low = contribute(j, vectors)
        if j == 0:
            pl.semaphore_wait(barrier, 3 * n_sub - 1 + N_Z - 1 + n_y - 1)
        each(1, n_sub, lambda k: rs_copy(j, sub_peer(k), sub).start())
        if j == 0:
            lax.fori_loop(0, table_hi.shape[0] // BUILD_ROWS, build, 0)
        gathered[j, sub] = contrib[j, sub]
        summed = apply(high, low, 0, nodes)
        each(1, n_sub, lambda k: rs_copy(j, sub_peer(k), sub_peer(k)).wait_recv())
        pools[j, 1, sub] = total(gathered.at[j], n_sub)
        each(1, n_sub, lambda k: ag_copy(j, 1, sub_peer(k), 1, sub).start())
        each(0, n_sub, lambda k: ag_copy(j, 0, k, 2, sub).start())
        each(0, n_sub, lambda k: ag_copy(j, 2, k, 0, sub).start())
        meanwhile()
        each(1, n_sub, lambda k: ag_copy(j, 1, sub_peer(k), 1, sub_peer(k)).wait_recv())
        for area in (1, 0, 2):
            if area != 1:
                each(0, n_sub, lambda k: ag_copy(j, area, k, area, k).wait_recv())
            high, low = split(pools[j, area].reshape(block, slots))
            summed = summed + apply(high, low, nodes + area * slots, slots)
        return summed

    def moments_zero():
        partial[0:block, 0:block] = outer(start_ref[...], start_ref[...])

    def moments_one():
        partial[0:block, block : 2 * block] = outer(start_ref[...], one_ref[...])
        partial[block : 2 * block, 0:block] = outer(one_ref[...], one_ref[...])

    def moments_two():
        partial[block : 2 * block, block : 2 * block] = outer(one_ref[...], two_ref[...])
        partial[2 * block : 3 * block, 0:block] = outer(two_ref[...], two_ref[...])

    one_ref[...] = affinity(0, start_ref[...], moments_zero)
    two_ref[...] = affinity(1, one_ref[...], moments_one)
    three = affinity(2, two_ref[...], moments_two)
    partial[2 * block : 3 * block, block : 2 * block] = outer(two_ref[...], three)

    each(1, n_sub, lambda k: part_copy(sub_peer(k), sub).start())
    part_in[sub] = partial[rows_of(sub), :]
    each(1, n_sub, lambda k: part_copy(sub_peer(k), sub_peer(k)).wait_recv())
    z_in[col] = total(part_in, n_sub)
    each(1, N_Z, lambda k: z_copy(z_peer(k), col).start())
    each(1, N_Z, lambda k: z_copy(z_peer(k), z_peer(k)).wait_recv())
    y_in[row] = total(z_in, N_Z)
    each(1, n_y, lambda k: y_copy(y_peer(k), row).start())
    each(1, n_y, lambda k: y_copy(y_peer(k), y_peer(k)).wait_recv())
    sums_ref[rows_of(sub), :] = total(y_in, n_y)
    each(1, n_sub, lambda k: out_copy(sub_peer(k), sub).start())
    each(1, n_sub, lambda k: out_copy(sub_peer(k), sub_peer(k)).wait_recv())

    for j in range(ROUNDS):
        each(1, n_sub, lambda k: rs_copy(j, sub_peer(k), sub).wait_send())
        each(1, n_sub, lambda k: ag_copy(j, 1, sub_peer(k), 1, sub).wait_send())
        each(0, n_sub, lambda k: ag_copy(j, 0, k, 2, sub).wait_send())
        each(0, n_sub, lambda k: ag_copy(j, 2, k, 0, sub).wait_send())
    each(1, n_sub, lambda k: part_copy(sub_peer(k), sub).wait_send())
    each(1, N_Z, lambda k: z_copy(z_peer(k), col).wait_send())
    each(1, n_y, lambda k: y_copy(y_peer(k), row).wait_send())
    each(1, n_sub, lambda k: out_copy(sub_peer(k), sub).wait_send())


def powers_and_sums(start, links, link_weight, pool_slot):
    n_dom = lax.axis_size("dom")
    n_sub = lax.axis_size("sub")
    n_y = n_dom // N_Z
    block, nodes = start.shape
    slots = SLOT_DEV * n_sub
    share = block // n_sub
    part = 3 * block // n_sub
    entries = nodes + 3 * slots
    vectors = jax.ShapeDtypeStruct((block, nodes), jnp.float32)
    f32 = jnp.float32
    return pl.pallas_call(
        functools.partial(sums_kernel, n_dom, n_sub),
        out_shape=(vectors, vectors, jax.ShapeDtypeStruct((3 * block, 2 * block), f32)),
        in_specs=[pl.BlockSpec(memory_space=VMEM)] * 4,
        out_specs=(pl.BlockSpec(memory_space=VMEM),) * 3,
        scratch_shapes=[
            VMEM((1, nodes), f32),
            VMEM((slots, nodes), jnp.bfloat16),
            VMEM((entries, nodes), jnp.bfloat16),
            VMEM((entries, nodes), jnp.bfloat16),
            VMEM((ROUNDS, n_sub, share, slots), f32),
            VMEM((ROUNDS, n_sub, share, slots), f32),
            VMEM((ROUNDS, 3, n_sub, share, slots), f32),
            VMEM((3 * block, 2 * block), f32),
            VMEM((n_sub, part, 2 * block), f32),
            VMEM((N_Z, part, 2 * block), f32),
            VMEM((n_y, part, 2 * block), f32),
            DMA((ROUNDS, n_sub)),
            DMA((ROUNDS, n_sub)),
            DMA((ROUNDS, 3, n_sub)),
            DMA((ROUNDS, 3, n_sub)),
            DMA((n_sub,)),
            DMA((n_sub,)),
            DMA((N_Z,)),
            DMA((N_Z,)),
            DMA((n_y,)),
            DMA((n_y,)),
            DMA((n_sub,)),
            DMA((n_sub,)),
        ],
        compiler_params=pltpu.CompilerParams(
            collective_id=0, has_side_effects=True, vmem_limit_bytes=32 * 1024 * 1024
        ),
        name="powers_and_sums",
    )(start, links, link_weight, pool_slot.reshape(1, nodes))


def product(left, right, dims):
    return lax.dot_general(
        left, right, (dims, ((), ())),
        precision=lax.Precision.HIGHEST, preferred_element_type=jnp.float32,
    )


def nn(left, right):
    return product(left, right, ((1,), (0,)))


def nt(left, right):
    return product(left, right, ((1,), (1,)))


def tn(left, right):
    return product(left, right, ((0,), (0,)))


def eye(size):
    rows = lax.broadcasted_iota(jnp.int32, (size, size), 0)
    cols = lax.broadcasted_iota(jnp.int32, (size, size), 1)
    return jnp.where(rows == cols, 1.0, 0.0)


def mean_with_transpose(matrix):
    return 0.5 * (matrix + matrix.T)


def cholesky_and_inverse(matrix):
    size = matrix.shape[0]
    tiles = size // SUBLANES
    wide = jnp.concatenate([matrix, eye(size)], axis=1)
    shape = (SUBLANES, 2 * size)
    rows = [wide[SUBLANES * i : SUBLANES * (i + 1), :] for i in range(tiles)]
    ids = lax.broadcasted_iota(jnp.int32, shape, 0)
    pivots = []
    for t in range(tiles):
        first = SUBLANES * t
        spread = {
            (i, k): jnp.broadcast_to(rows[i][:, first + k : first + k + 1], shape)
            for i in range(t, tiles)
            for k in range(SUBLANES)
        }
        for k in range(SUBLANES):
            inverse = 1.0 / jnp.broadcast_to(spread[t, k][k : k + 1, :], shape)
            row = jnp.broadcast_to(rows[t][k : k + 1, :], shape) * inverse
            ahead = {
                c: jnp.broadcast_to(spread[t, c][k : k + 1, :], shape) * inverse
                for c in range(k + 1, SUBLANES)
            }
            for i in range(t, tiles):
                factor = spread[i, k]
                if i == t:
                    factor = jnp.where(ids > k, factor, 0.0)
                rows[i] = rows[i] - factor * row
                for c in range(k + 1, SUBLANES):
                    spread[i, c] = spread[i, c] - factor * ahead[c]
        pivot = spread[t, 0]
        for k in range(1, SUBLANES):
            pivot = jnp.where(ids == k, spread[t, k], pivot)
        rows[t] = rows[t] * lax.rsqrt(pivot)
    result = jnp.concatenate(rows, axis=0)
    upper = result[:, :size]
    row_ids = lax.broadcasted_iota(jnp.int32, (size, size), 0)
    col_ids = lax.broadcasted_iota(jnp.int32, (size, size), 1)
    return jnp.where(col_ids >= row_ids, upper, 0.0), result[:, size:]


def filtered(reduced, first):
    half = 0.5 * (reduced + eye(reduced.shape[0]))
    square = nn(half, half)
    return nn(square, first(square))


def ritz_step_one(m0, m1, m2, m3):
    block = m0.shape[0]
    zero = jnp.zeros_like(m0)
    upper, inv_first = cholesky_and_inverse(m0)
    below = nt(m1, inv_first)
    _, inv_second = cholesky_and_inverse(m2 - nt(below, below))
    inv_below = -nn(inv_second, nn(below, inv_first))
    inverse = jnp.concatenate(
        [
            jnp.concatenate([inv_first, zero], axis=1),
            jnp.concatenate([inv_below, inv_second], axis=1),
        ],
        axis=0,
    )
    mixed = jnp.concatenate(
        [jnp.concatenate([m1, m2], axis=1), jnp.concatenate([m2, m3], axis=1)], axis=0
    )
    reduced = nt(nn(inverse, mixed), inverse)
    tilted = filtered(reduced, lambda square: nn(square[:, :block], upper))
    _, normal = cholesky_and_inverse(tn(tilted, tilted))
    orthonormal = nt(tilted, normal)
    coeffs = tn(inverse, orthonormal)
    theta = tn(orthonormal, nn(reduced, orthonormal))
    return coeffs[:block], coeffs[block:], theta


def ritz_step_two(moments, head, tail, theta):
    block = head.shape[0]
    zero = jnp.zeros_like(head)

    def hankel(first):
        return jnp.concatenate(
            [
                jnp.concatenate([moments[first + i + j] for j in range(3)], axis=1)
                for i in range(3)
            ],
            axis=0,
        )

    gram, mixed = hankel(0), hankel(1)
    current = jnp.concatenate([head, tail, zero], axis=0)
    search = jnp.concatenate([zero, tail, zero], axis=0)
    residual = jnp.concatenate([zero, head, tail], axis=0) - nn(current, theta)
    search = search - nn(current, tn(current, nn(gram, search)))
    _, normal = cholesky_and_inverse(tn(search, nn(gram, search)))
    search = nt(search, normal)
    residual = residual - nn(search, tn(search, nn(gram, residual)))
    _, normal = cholesky_and_inverse(tn(residual, nn(gram, residual)))
    residual = nt(residual, normal)
    basis = jnp.concatenate([current, search, residual], axis=1)
    reduced = tn(basis, nn(mixed, basis))
    tilted = filtered(reduced, lambda square: square[:, :block])
    _, normal = cholesky_and_inverse(tn(tilted, tilted))
    orthonormal = nt(tilted, normal)
    ritz = tn(orthonormal, nn(reduced, orthonormal))
    return nn(basis, orthonormal), ritz


def ritz_kernel(scale, sums_ref, start_ref, one_ref, two_ref, eigen_ref, ritz_ref):
    block = start_ref.shape[0]
    moments = [
        mean_with_transpose(
            sums_ref[r * block : (r + 1) * block, c * block : (c + 1) * block] * scale
        )
        for r in range(3)
        for c in range(2)
    ]
    head, tail, theta = ritz_step_one(*moments[:4])
    weights, ritz = ritz_step_two(moments, head, tail, theta)
    ritz_ref[...] = ritz
    powers = jnp.concatenate([start_ref[...], one_ref[...], two_ref[...]], axis=0)
    eigen_ref[...] = tn(weights, powers)


def per_device(start, links, link_weight, pool_slot):
    block, nodes = start.shape
    node_count = nodes * lax.axis_size("dom") * lax.axis_size("sub")
    one, two, sums = powers_and_sums(start, links, link_weight, pool_slot)
    return pl.pallas_call(
        functools.partial(ritz_kernel, 1.0 / node_count),
        out_shape=(
            jax.ShapeDtypeStruct((block, nodes), jnp.float32),
            jax.ShapeDtypeStruct((block, block), jnp.float32),
        ),
        in_specs=[pl.BlockSpec(memory_space=VMEM)] * 4,
        out_specs=(pl.BlockSpec(memory_space=VMEM),) * 2,
        compiler_params=pltpu.CompilerParams(vmem_limit_bytes=32 * 1024 * 1024),
        name="ritz_steps",
    )(sums, start, one, two)


def solution(mesh):
    placed = (
        P(None, ("dom", "sub")),
        P(None, ("dom", "sub")),
        P(None, ("dom", "sub")),
        P(("dom", "sub")),
    )
    return jax.shard_map(
        per_device,
        mesh=mesh,
        in_specs=placed,
        out_specs=(P(None, ("dom", "sub")), P()),
        check_vma=False,
    )
```

```python
import functools

import jax
import jax.numpy as jnp
from jax import lax
from jax.experimental import pallas as pl
from jax.experimental.pallas import tpu as pltpu
from jax.sharding import PartitionSpec as P

MESH = pl.DeviceIdType.MESH
VMEM = pltpu.VMEM
DMA = pltpu.SemaphoreType.DMA
SLOT_DEV = 64
ROUNDS = 3
BUILD_ROWS = 64
N_Z = 12
SUBLANES = 8
LANES = 128
WIDTHS = (2 * LANES, LANES, LANES)


def split(values):
    high = values.astype(jnp.bfloat16)
    low = (values - high.astype(jnp.float32)).astype(jnp.bfloat16)
    return high, low


def product(left, right, dims):
    return lax.dot_general(
        left, right, (dims, ((), ())),
        precision=lax.Precision.HIGHEST, preferred_element_type=jnp.float32,
    )


def nn(left, right):
    return product(left, right, ((1,), (0,)))


def nt(left, right):
    return product(left, right, ((1,), (1,)))


def tn(left, right):
    return product(left, right, ((0,), (0,)))


def eye(size):
    rows = lax.broadcasted_iota(jnp.int32, (size, size), 0)
    cols = lax.broadcasted_iota(jnp.int32, (size, size), 1)
    return jnp.where(rows == cols, 1.0, 0.0)


def mean_with_transpose(matrix):
    return 0.5 * (matrix + matrix.T)


def cholesky_and_inverse(matrix):
    size = matrix.shape[0]
    width = 2 * size
    rows = jnp.concatenate([matrix, eye(size)], axis=1)
    ids = lax.broadcasted_iota(jnp.int32, (size, width), 0)
    done = []
    for first in range(0, size, SUBLANES):
        left = size - first
        tile = (SUBLANES, width)
        spread = [
            jnp.broadcast_to(rows[:, first + k : first + k + 1], (left, width))
            for k in range(SUBLANES)
        ]
        for k in range(SUBLANES):
            inverse = 1.0 / jnp.broadcast_to(spread[k][k : k + 1, :], tile)
            factor = jnp.where(ids[:left] > k, spread[k], 0.0)

            def eliminate(values):
                pivot_row = jnp.broadcast_to(values[k : k + 1, :], tile) * inverse
                return values - factor * jnp.concatenate([pivot_row] * (left // SUBLANES), axis=0)

            rows = eliminate(rows)
            for c in range(k + 1, SUBLANES):
                spread[c] = eliminate(spread[c])
        pivot = spread[0][:SUBLANES]
        for k in range(1, SUBLANES):
            pivot = jnp.where(ids[:SUBLANES] == k, spread[k][:SUBLANES], pivot)
        done.append(rows[:SUBLANES] * lax.rsqrt(pivot))
        rows = rows[SUBLANES:]
    result = jnp.concatenate(done, axis=0)
    upper = result[:, :size]
    row_ids = lax.broadcasted_iota(jnp.int32, (size, size), 0)
    col_ids = lax.broadcasted_iota(jnp.int32, (size, size), 1)
    return jnp.where(col_ids >= row_ids, upper, 0.0), result[:, size:]


def blocks(rows):
    return jnp.concatenate([jnp.concatenate(row, axis=1) for row in rows], axis=0)


def filtered(reduced, first):
    half = 0.5 * (reduced + eye(reduced.shape[0]))
    square = nn(half, half)
    return nn(square, first(square))


def factor_one(m0, m1, m2):
    upper, first = cholesky_and_inverse(m0)
    below = nt(m1, first)
    return upper, first, below, m2 - nt(below, below)


def inverse_one(first, below, rest):
    _, second = cholesky_and_inverse(rest)
    corner = -nn(second, nn(below, first))
    return blocks([[first, jnp.zeros_like(first)], [corner, second]])


def filter_one(inverse, upper, m1, m2, m3):
    block = upper.shape[0]
    reduced = nt(nn(inverse, blocks([[m1, m2], [m2, m3]])), inverse)
    tilted = filtered(reduced, lambda square: nn(square[:, :block], upper))
    return reduced, tilted, tn(tilted, tilted)


def ritz_one(inverse, reduced, tilted, gram):
    _, normal = cholesky_and_inverse(gram)
    orthonormal = nt(tilted, normal)
    coeffs = tn(inverse, orthonormal)
    return coeffs, tn(orthonormal, nn(reduced, orthonormal))


def basis_two(coeffs, theta, moments):
    m0, m1, m2, m3, m4 = moments
    block = theta.shape[0]
    head, tail = coeffs[:block], coeffs[block:]
    zero = jnp.zeros_like(head)
    gram = blocks([[m0, m1, m2], [m1, m2, m3], [m2, m3, m4]])
    current = jnp.concatenate([head, tail, zero], axis=0)
    search = jnp.concatenate([zero, tail, zero], axis=0)
    residual = jnp.concatenate([zero, head, tail], axis=0) - nn(current, theta)
    gram_current = nn(gram, current)
    search = search - nn(current, tn(gram_current, search))
    gram_search = nn(gram, search)
    _, normal = cholesky_and_inverse(tn(search, gram_search))
    search = nt(search, normal)
    gram_search = nt(gram_search, normal)
    residual = residual - nn(search, tn(gram_search, residual))
    _, normal = cholesky_and_inverse(tn(residual, nn(gram, residual)))
    residual = nt(residual, normal)
    basis = jnp.concatenate([current, search, residual], axis=1)
    mixed = blocks([[m1, m2, m3], [m2, m3, m4], [m3, m4, zero]])
    return basis, tn(basis, nn(mixed, basis))


def ritz_kernel(scale, sums_ref, basis_ref, partial_ref, rotated_ref, eigen_ref, ritz_ref):
    block = ritz_ref.shape[0]
    last = mean_with_transpose(sums_ref[:, :block] * scale)
    tail = basis_ref[2 * block :, 2 * block :]
    zero = jnp.zeros((block, block), jnp.float32)
    corner = tn(tail, nn(last, tail))
    reduced = partial_ref[...] + blocks(
        [[zero, zero, zero], [zero, zero, zero], [zero, zero, corner]]
    )
    tilted = filtered(reduced, lambda square: square[:, :block])
    _, normal = cholesky_and_inverse(tn(tilted, tilted))
    turned = tn(tilted, rotated_ref[...])
    projected = tn(tilted, nn(reduced, tilted))
    eigen_ref[...] = nn(normal, turned)
    ritz_ref[...] = nt(nn(normal, projected), normal)


def each(low, high, body):
    lax.fori_loop(low, high, lambda k, c: (body(k), c)[1], 0)


def far_first(count):
    return sorted(range(1, count), key=lambda k: -min(k, count - k))


def sums_kernel(
    n_dom,
    n_sub,
    start_ref,
    links_ref,
    weight_ref,
    slot_ref,
    basis_ref,
    partial_ref,
    rotated_ref,
    last_ref,
    one_ref,
    two_ref,
    root_ref,
    place_ref,
    table_hi,
    table_lo,
    contrib,
    gathered,
    pools,
    own_a,
    own_b,
    own_c,
    part_a,
    part_b,
    part_c,
    z_a,
    z_b,
    z_c,
    y_a,
    y_b,
    y_c,
    sums_a,
    sums_b,
    rs_send,
    rs_recv,
    ag_send,
    ag_recv,
    part_send,
    part_recv,
    z_send,
    z_recv,
    y_send,
    y_recv,
    out_send,
    out_recv,
):
    dom = lax.axis_index("dom")
    sub = lax.axis_index("sub")
    n_y = n_dom // N_Z
    row = lax.div(dom, N_Z)
    col = lax.rem(dom, N_Z)
    block = start_ref.shape[0]
    nodes = start_ref.shape[1]
    slots = place_ref.shape[0]
    share = block // n_sub
    scale = 1.0 / (nodes * n_dom * n_sub)
    own = (own_a, own_b, own_c)
    part_in = (part_a, part_b, part_c)
    z_in = (z_a, z_b, z_c)
    y_in = (y_a, y_b, y_c)
    sums = (sums_a, sums_b, last_ref)

    def sub_peer(k):
        return lax.rem(sub + k, n_sub)

    def dom_peer(area):
        return lax.rem(dom + (area + n_dom - 1), n_dom)

    def z_peer(k):
        return lax.rem(col + k, N_Z)

    def y_peer(k):
        return lax.rem(row + k, n_y)

    def remote(src, dst, send, recv, d, s):
        return pltpu.make_async_remote_copy(
            src_ref=src, dst_ref=dst, send_sem=send, recv_sem=recv,
            device_id=(d, s), device_id_type=MESH,
        )

    barrier = pltpu.get_barrier_semaphore()

    def greet(d, s):
        pl.semaphore_signal(barrier, inc=1, device_id=(d, s), device_id_type=MESH)

    for k in far_first(n_sub):
        greet(dom, sub_peer(k))
    for k in range(n_sub):
        greet(dom_peer(0), k)
        greet(dom_peer(2), k)
    for k in far_first(N_Z):
        greet(row * N_Z + z_peer(k), sub)
    for k in far_first(n_y):
        greet(y_peer(k) * N_Z + col, sub)

    def rs_copy(j, peer, at):
        return remote(contrib.at[j, peer], gathered.at[j, at],
                      rs_send.at[j, peer], rs_recv.at[j, at], dom, peer)

    def ag_copy(j, to, peer, area, at):
        return remote(pools.at[j, 1, sub], pools.at[j, area, at],
                      ag_send.at[j, to, peer], ag_recv.at[j, area, at], dom_peer(to), peer)

    def rows_of(p):
        return pl.ds(pl.multiple_of(p * share, share), share)

    def part_copy(b, peer, at):
        return remote(own[b].at[rows_of(peer)], part_in[b].at[at],
                      part_send.at[b, peer], part_recv.at[b, at], dom, peer)

    def z_copy(b, peer, at):
        return remote(z_in[b].at[col], z_in[b].at[at],
                      z_send.at[b, peer], z_recv.at[b, at], row * N_Z + peer, sub)

    def y_copy(b, peer, at):
        return remote(y_in[b].at[row], y_in[b].at[at],
                      y_send.at[b, peer], y_recv.at[b, at], peer * N_Z + col, sub)

    def out_copy(b, peer, at):
        return remote(sums[b].at[rows_of(sub)], sums[b].at[rows_of(at)],
                      out_send.at[b, peer], out_recv.at[b, at], dom, peer)

    def total(ref, count):
        result = ref[0]
        for k in range(1, count):
            result = result + ref[k]
        return result

    def sum_begin(b):
        for k in far_first(n_sub):
            part_copy(b, sub_peer(k), sub).start()
        part_in[b][sub] = own[b][rows_of(sub), :]

    def sum_along_z(b):
        for k in far_first(n_sub)[::-1]:
            part_copy(b, sub_peer(k), sub_peer(k)).wait_recv()
        z_in[b][col] = total(part_in[b], n_sub)
        for k in far_first(N_Z):
            z_copy(b, z_peer(k), col).start()

    def sum_along_y(b):
        for k in far_first(N_Z)[::-1]:
            z_copy(b, z_peer(k), z_peer(k)).wait_recv()
        y_in[b][row] = total(z_in[b], N_Z)
        for k in far_first(n_y):
            y_copy(b, y_peer(k), row).start()

    def sum_back(b):
        for k in far_first(n_y)[::-1]:
            y_copy(b, y_peer(k), y_peer(k)).wait_recv()
        sums[b][rows_of(sub), :] = total(y_in[b], n_y)
        for k in far_first(n_sub):
            out_copy(b, sub_peer(k), sub).start()

    def sum_end(b):
        for k in far_first(n_sub)[::-1]:
            out_copy(b, sub_peer(k), sub_peer(k)).wait_recv()

    def sum_sent(b):
        each(1, n_sub, lambda k: part_copy(b, sub_peer(k), sub).wait_send())
        each(1, N_Z, lambda k: z_copy(b, z_peer(k), col).wait_send())
        each(1, n_y, lambda k: y_copy(b, y_peer(k), row).wait_send())
        each(1, n_sub, lambda k: out_copy(b, sub_peer(k), sub).wait_send())

    def rs_sent(j):
        each(1, n_sub, lambda k: rs_copy(j, sub_peer(k), sub).wait_send())

    def ag_sent(j):
        each(1, n_sub, lambda k: ag_copy(j, 1, sub_peer(k), 1, sub).wait_send())
        each(0, n_sub, lambda k: ag_copy(j, 0, k, 2, sub).wait_send())
        each(0, n_sub, lambda k: ag_copy(j, 2, k, 0, sub).wait_send())

    root_ref[...] = lax.rsqrt(jnp.sum(weight_ref[...], axis=0, keepdims=True))

    def place(i, carry):
        base = pl.multiple_of(i * BUILD_ROWS, BUILD_ROWS)
        ids = base + lax.broadcasted_iota(jnp.int32, (BUILD_ROWS, nodes), 0)
        place_ref[pl.ds(base, BUILD_ROWS), :] = jnp.where(
            ids == slot_ref[...], 1.0, 0.0
        ).astype(jnp.bfloat16)
        return carry

    lax.fori_loop(0, slots // BUILD_ROWS, place, 0)

    def build(i, carry):
        base = pl.multiple_of(i * BUILD_ROWS, BUILD_ROWS)
        ids = base + lax.broadcasted_iota(jnp.int32, (BUILD_ROWS, nodes), 0)
        summed = jnp.zeros((BUILD_ROWS, nodes), jnp.float32)
        for k in range(links_ref.shape[0]):
            summed = summed + jnp.where(
                ids == links_ref[k : k + 1, :], weight_ref[k : k + 1, :], 0.0
            )
        high, low = split(summed * root_ref[...])
        table_hi[pl.ds(base, BUILD_ROWS), :] = high
        table_lo[pl.ds(base, BUILD_ROWS), :] = low
        return carry

    def contribute(j, vectors):
        high, low = split(root_ref[...] * vectors)
        spread = lax.dot_general(
            jnp.concatenate([high, low], axis=0),
            place_ref[...],
            (((1,), (1,)), ((), ())),
            preferred_element_type=jnp.float32,
        )
        contrib[j] = (spread[:block] + spread[block:]).reshape(n_sub, share, slots)
        return high, low

    def apply(high, low, first, count):
        upper = jnp.dot(
            jnp.concatenate([high, low], axis=0),
            table_hi[first : first + count, :],
            preferred_element_type=jnp.float32,
        )
        lower = jnp.dot(
            high, table_lo[first : first + count, :], preferred_element_type=jnp.float32
        )
        return upper[:block] + upper[block:] + lower

    def affinity(j, vectors, while_reduced, while_gathered):
        high, low = contribute(j, vectors)
        if j == 0:
            pl.semaphore_wait(barrier, 3 * n_sub - 1 + N_Z - 1 + n_y - 1)
        for k in far_first(n_sub):
            rs_copy(j, sub_peer(k), sub).start()
        gathered[j, sub] = contrib[j, sub]
        while_reduced()
        summed = apply(high, low, 0, nodes)
        for k in far_first(n_sub)[::-1]:
            rs_copy(j, sub_peer(k), sub_peer(k)).wait_recv()
        pools[j, 1, sub] = total(gathered.at[j], n_sub)
        for k in far_first(n_sub) + [0]:
            ag_copy(j, 0, sub_peer(k), 2, sub).start()
            ag_copy(j, 2, sub_peer(k), 0, sub).start()
        for k in far_first(n_sub):
            ag_copy(j, 1, sub_peer(k), 1, sub).start()
        while_gathered()
        for k in range(1, n_sub):
            ag_copy(j, 1, sub_peer(k), 1, sub_peer(k)).wait_recv()
        for area in (1, 0, 2):
            if area != 1:
                for k in range(n_sub):
                    ag_copy(j, area, k, area, k).wait_recv()
            high, low = split(pools[j, area].reshape(block, slots))
            summed = summed + apply(high, low, nodes + area * slots, slots)
        return summed

    def build_table():
        lax.fori_loop(0, table_hi.shape[0] // BUILD_ROWS, build, 0)

    def moments_first():
        own_a[:, 0:block] = nt(start_ref[...], start_ref[...])
        own_a[:, 3 * block :] = jnp.zeros((block, block), jnp.float32)
        own_c[:, block:] = jnp.zeros((block, block), jnp.float32)
        rs_sent(0)

    def moments_second():
        own_a[:, block : 2 * block] = nt(start_ref[...], one_ref[...])
        own_a[:, 2 * block : 3 * block] = nt(one_ref[...], one_ref[...])
        sum_begin(0)
        ag_sent(0)

    def second_gathered():
        sum_along_z(0)
        rs_sent(1)

    def moments_third():
        own_b[:, 0:block] = nt(one_ref[...], two_ref[...])
        own_b[:, block:] = nt(two_ref[...], two_ref[...])
        sum_begin(1)
        sum_along_y(0)
        ag_sent(1)

    def third_gathered():
        sum_back(0)
        sum_along_z(1)
        rs_sent(2)

    one_ref[...] = affinity(0, start_ref[...], build_table, moments_first)
    two_ref[...] = affinity(1, one_ref[...], moments_second, second_gathered)
    three = affinity(2, two_ref[...], moments_third, third_gathered)
    own_c[:, 0:block] = nt(two_ref[...], three)

    def moment(b, c):
        return mean_with_transpose(sums[b][:, c * block : (c + 1) * block] * scale)

    sum_begin(2)
    sum_along_y(1)
    sum_end(0)
    m0, m1, m2 = moment(0, 0), moment(0, 1), moment(0, 2)
    upper, first, below, rest = factor_one(m0, m1, m2)
    sum_along_z(2)
    sum_back(1)
    inverse = inverse_one(first, below, rest)
    ag_sent(2)
    sum_sent(0)
    sum_end(1)
    m3, m4 = moment(1, 0), moment(1, 1)
    reduced, tilted, gram = filter_one(inverse, upper, m1, m2, m3)
    sum_along_y(2)
    coeffs, theta = ritz_one(inverse, reduced, tilted, gram)
    sum_back(2)
    basis, partial = basis_two(coeffs, theta, (m0, m1, m2, m3, m4))
    basis_ref[...] = basis
    partial_ref[...] = partial
    rotated_ref[...] = tn(
        basis, jnp.concatenate([start_ref[...], one_ref[...], two_ref[...]], axis=0)
    )
    sum_sent(1)
    sum_sent(2)
    sum_end(2)


def per_device(start, links, link_weight, pool_slot):
    n_dom = lax.axis_size("dom")
    n_sub = lax.axis_size("sub")
    n_y = n_dom // N_Z
    block, nodes = start.shape
    slots = SLOT_DEV * n_sub
    share = block // n_sub
    entries = nodes + 3 * slots
    f32 = jnp.float32
    vmem = pl.BlockSpec(memory_space=VMEM)
    limit = 32 * 1024 * 1024

    def array(*shape):
        return jax.ShapeDtypeStruct(shape, f32)

    def buffers(*shape):
        return [VMEM(shape + (width,), f32) for width in WIDTHS]

    basis, partial, rotated, last = pl.pallas_call(
        functools.partial(sums_kernel, n_dom, n_sub),
        out_shape=(
            array(3 * block, 3 * block),
            array(3 * block, 3 * block),
            array(3 * block, nodes),
            array(block, WIDTHS[2]),
        ),
        in_specs=[vmem] * 4,
        out_specs=(vmem,) * 4,
        scratch_shapes=[
            VMEM((block, nodes), f32),
            VMEM((block, nodes), f32),
            VMEM((1, nodes), f32),
            VMEM((slots, nodes), jnp.bfloat16),
            VMEM((entries, nodes), jnp.bfloat16),
            VMEM((entries, nodes), jnp.bfloat16),
            VMEM((ROUNDS, n_sub, share, slots), f32),
            VMEM((ROUNDS, n_sub, share, slots), f32),
            VMEM((ROUNDS, 3, n_sub, share, slots), f32),
            *buffers(block),
            *buffers(n_sub, share),
            *buffers(N_Z, share),
            *buffers(n_y, share),
            *buffers(block)[:2],
            DMA((ROUNDS, n_sub)),
            DMA((ROUNDS, n_sub)),
            DMA((ROUNDS, 3, n_sub)),
            DMA((ROUNDS, 3, n_sub)),
            *[DMA((len(WIDTHS), size)) for size in (n_sub, N_Z, n_y, n_sub) for _ in range(2)],
        ],
        compiler_params=pltpu.CompilerParams(
            collective_id=0, has_side_effects=True, vmem_limit_bytes=limit
        ),
        name="powers_and_sums",
    )(start, links, link_weight, pool_slot.reshape(1, nodes))
    return pl.pallas_call(
        functools.partial(ritz_kernel, 1.0 / (nodes * n_dom * n_sub)),
        out_shape=(array(block, nodes), array(block, block)),
        in_specs=[vmem] * 4,
        out_specs=(vmem,) * 2,
        compiler_params=pltpu.CompilerParams(vmem_limit_bytes=limit),
        name="ritz_steps",
    )(last, basis, partial, rotated)


def solution(mesh):
    placed = (
        P(None, ("dom", "sub")),
        P(None, ("dom", "sub")),
        P(None, ("dom", "sub")),
        P(("dom", "sub")),
    )
    return jax.shard_map(
        per_device,
        mesh=mesh,
        in_specs=placed,
        out_specs=(P(None, ("dom", "sub")), P()),
        check_vma=False,
    )
```

```python
import functools

import jax
import jax.numpy as jnp
from jax import lax
from jax.experimental import pallas as pl
from jax.experimental.pallas import tpu as pltpu
from jax.sharding import PartitionSpec as P

MESH = pl.DeviceIdType.MESH
VMEM = pltpu.VMEM
DMA = pltpu.SemaphoreType.DMA
SLOT_DEV = 64
ROUNDS = 3
BUILD_ROWS = 64
N_Z = 12
SUBLANES = 8
LANES = 128
WIDTHS = (2 * LANES, LANES, LANES)


def split(values):
    high = values.astype(jnp.bfloat16)
    low = (values - high.astype(jnp.float32)).astype(jnp.bfloat16)
    return high, low


def product(left, right, dims):
    return lax.dot_general(
        left, right, (dims, ((), ())),
        precision=lax.Precision.HIGHEST, preferred_element_type=jnp.float32,
    )


def nn(left, right):
    return product(left, right, ((1,), (0,)))


def nt(left, right):
    return product(left, right, ((1,), (1,)))


def tn(left, right):
    return product(left, right, ((0,), (0,)))


def eye(size):
    rows = lax.broadcasted_iota(jnp.int32, (size, size), 0)
    cols = lax.broadcasted_iota(jnp.int32, (size, size), 1)
    return jnp.where(rows == cols, 1.0, 0.0)


def mean_with_transpose(matrix):
    return 0.5 * (matrix + matrix.T)


def cholesky_and_inverse(matrix):
    size = matrix.shape[0]
    width = 2 * size
    rows = jnp.concatenate([matrix, eye(size)], axis=1)
    ids = lax.broadcasted_iota(jnp.int32, (size, width), 0)
    done = []
    for first in range(0, size, SUBLANES):
        left = size - first
        tile = (SUBLANES, width)
        spread = [
            jnp.broadcast_to(rows[:, first + k : first + k + 1], (left, width))
            for k in range(SUBLANES)
        ]
        for k in range(SUBLANES):
            inverse = 1.0 / jnp.broadcast_to(spread[k][k : k + 1, :], tile)
            factor = jnp.where(ids[:left] > k, spread[k], 0.0)

            def eliminate(values):
                pivot_row = jnp.broadcast_to(values[k : k + 1, :], tile) * inverse
                return values - factor * jnp.concatenate([pivot_row] * (left // SUBLANES), axis=0)

            rows = eliminate(rows)
            for c in range(k + 1, SUBLANES):
                spread[c] = eliminate(spread[c])
        pivot = spread[0][:SUBLANES]
        for k in range(1, SUBLANES):
            pivot = jnp.where(ids[:SUBLANES] == k, spread[k][:SUBLANES], pivot)
        done.append(rows[:SUBLANES] * lax.rsqrt(pivot))
        rows = rows[SUBLANES:]
    result = jnp.concatenate(done, axis=0)
    upper = result[:, :size]
    row_ids = lax.broadcasted_iota(jnp.int32, (size, size), 0)
    col_ids = lax.broadcasted_iota(jnp.int32, (size, size), 1)
    return jnp.where(col_ids >= row_ids, upper, 0.0), result[:, size:]


def blocks(rows):
    return jnp.concatenate([jnp.concatenate(row, axis=1) for row in rows], axis=0)


def filtered(reduced, first):
    half = 0.5 * (reduced + eye(reduced.shape[0]))
    square = nn(half, half)
    return nn(square, first(square))


def factor_one(m0, m1, m2):
    upper, first = cholesky_and_inverse(m0)
    below = nt(m1, first)
    return upper, first, below, m2 - nt(below, below)


def inverse_one(first, below, rest):
    _, second = cholesky_and_inverse(rest)
    corner = -nn(second, nn(below, first))
    return blocks([[first, jnp.zeros_like(first)], [corner, second]])


def filter_one(inverse, upper, m1, m2, m3):
    block = upper.shape[0]
    reduced = nt(nn(inverse, blocks([[m1, m2], [m2, m3]])), inverse)
    tilted = filtered(reduced, lambda square: nn(square[:, :block], upper))
    return tilted, tn(tilted, tilted)


def hankel(moments):
    return blocks([moments[i : i + 3] for i in range(3)])


def diagonal(part, count):
    zero = jnp.zeros_like(part)
    return blocks([[part if i == j else zero for j in range(count)] for i in range(count)])


def ritz_one(inverse, tilted, gram, moments, powers):
    block = gram.shape[0]
    coeffs = tn(inverse, tilted)
    head, tail = coeffs[:block], coeffs[block:]
    zero = jnp.zeros_like(head)
    spanned = blocks([[zero, zero, head], [tail, head, tail], [zero, tail, zero]])
    _, normal = cholesky_and_inverse(gram)
    products = tn(spanned, nn(hankel(moments), spanned[:, : 2 * block]))
    mixed = tn(spanned, nn(hankel(moments[1:] + [zero]), spanned))
    rotated = tn(spanned, powers)
    thrice = diagonal(normal, 3)
    return (
        nt(tail, normal),
        nt(nn(thrice, products), diagonal(normal, 2)),
        nt(nn(thrice, mixed), thrice),
        nn(thrice, rotated),
    )


def residual_and_search(products):
    block = products.shape[1] // 2
    along = products[2 * block :]
    return along, products[: 2 * block] - tn(along, along)


def eliminate_search(along, left):
    block = along.shape[0]
    shared, theta = along[:, :block], along[:, block:]
    _, normal = cholesky_and_inverse(left[:block, :block])
    overlap = nn(normal, left[:block, block:])
    return normal, overlap, left[block:, block:] - tn(overlap, overlap), shared, theta


def basis_two(normal, overlap, rest, shared, theta, mixed, rotated):
    block = rest.shape[0]
    zero = jnp.zeros_like(rest)
    _, last = cholesky_and_inverse(rest)
    search = normal.T
    along = nn(shared, search)
    turn = blocks(
        [
            [zero, search, -nn(search, overlap)],
            [zero, zero, eye(block)],
            [eye(block), -along, nn(along, overlap) - theta],
        ]
    )
    mixed = tn(turn, nn(mixed, turn))
    rotated = tn(turn, rotated)
    above, below = mixed[: 2 * block], nn(last, mixed[2 * block :])
    reduced = blocks(
        [
            [above[:, : 2 * block], nt(above[:, 2 * block :], last)],
            [below[:, : 2 * block], nt(below[:, 2 * block :], last)],
        ]
    )
    rotated = jnp.concatenate([rotated[: 2 * block], nn(last, rotated[2 * block :])], axis=0)
    return last, reduced, rotated


def ritz_kernel(scale, sums_ref, tail_ref, partial_ref, rotated_ref, eigen_ref, ritz_ref):
    block = ritz_ref.shape[0]
    last = mean_with_transpose(sums_ref[:, :block] * scale)
    tail = tail_ref[...]
    zero = jnp.zeros((block, block), jnp.float32)
    corner = tn(tail, nn(last, tail))
    reduced = partial_ref[...] + blocks(
        [[zero, zero, zero], [zero, zero, zero], [zero, zero, corner]]
    )
    tilted = filtered(reduced, lambda square: square[:, :block])
    _, normal = cholesky_and_inverse(tn(tilted, tilted))
    turned = tn(tilted, rotated_ref[...])
    projected = tn(tilted, nn(reduced, tilted))
    eigen_ref[...] = nn(normal, turned)
    ritz_ref[...] = nt(nn(normal, projected), normal)


def far_first(count):
    return sorted(range(1, count), key=lambda k: -min(k, count - k))


def sums_kernel(
    n_dom,
    n_sub,
    start_ref,
    links_ref,
    weight_ref,
    slot_ref,
    tail_ref,
    partial_ref,
    rotated_ref,
    last_ref,
    one_ref,
    two_ref,
    root_ref,
    place_ref,
    table_hi,
    table_lo,
    contrib,
    gathered,
    pools,
    own_a,
    own_b,
    own_c,
    part_a,
    part_b,
    part_c,
    z_a,
    z_b,
    z_c,
    y_a,
    y_b,
    y_c,
    sums_a,
    sums_b,
    rs_send,
    rs_recv,
    ag_send,
    ag_recv,
    part_send,
    part_recv,
    z_send,
    z_recv,
    y_send,
    y_recv,
    out_send,
    out_recv,
):
    dom = lax.axis_index("dom")
    sub = lax.axis_index("sub")
    n_y = n_dom // N_Z
    row = lax.div(dom, N_Z)
    col = lax.rem(dom, N_Z)
    block = start_ref.shape[0]
    nodes = start_ref.shape[1]
    slots = place_ref.shape[0]
    share = block // n_sub
    scale = 1.0 / (nodes * n_dom * n_sub)
    own = (own_a, own_b, own_c)
    part_in = (part_a, part_b, part_c)
    z_in = (z_a, z_b, z_c)
    y_in = (y_a, y_b, y_c)
    sums = (sums_a, sums_b, last_ref)

    def sub_peer(k):
        return lax.rem(sub + k, n_sub)

    def dom_peer(area):
        return lax.rem(dom + (area + n_dom - 1), n_dom)

    def z_peer(k):
        return lax.rem(col + k, N_Z)

    def y_peer(k):
        return lax.rem(row + k, n_y)

    def remote(src, dst, send, recv, d, s):
        return pltpu.make_async_remote_copy(
            src_ref=src, dst_ref=dst, send_sem=send, recv_sem=recv,
            device_id=(d, s), device_id_type=MESH,
        )

    barrier = pltpu.get_barrier_semaphore()

    def greet(d, s):
        pl.semaphore_signal(barrier, inc=1, device_id=(d, s), device_id_type=MESH)

    for k in far_first(N_Z):
        greet(row * N_Z + z_peer(k), sub)
    for k in far_first(n_y):
        greet(y_peer(k) * N_Z + col, sub)
    for k in far_first(n_sub) + [0]:
        greet(dom_peer(0), sub_peer(k))
        greet(dom_peer(2), sub_peer(k))
    for k in far_first(n_sub):
        greet(dom, sub_peer(k))

    def bulk(ref, send, recv):
        return remote(ref, ref, send, recv, dom, sub_peer(1))

    def rs_copy(j, peer):
        return remote(contrib.at[j, peer], gathered.at[j, sub],
                      rs_send.at[j], rs_recv.at[j], dom, peer)

    def rs_all(j):
        return bulk(gathered.at[j, 0 : n_sub - 1], rs_send.at[j], rs_recv.at[j])

    def ag_copy(j, to, peer, area):
        return remote(pools.at[j, 1, sub], pools.at[j, area, sub],
                      ag_send.at[j, to], ag_recv.at[j, area], dom_peer(to), peer)

    def ag_all(j, area):
        some = pools.at[j, area, 0 : n_sub - 1] if area == 1 else pools.at[j, area]
        return bulk(some, ag_send.at[j, area], ag_recv.at[j, area])

    def rows_of(p):
        return pl.ds(pl.multiple_of(p * share, share), share)

    def part_copy(b, peer):
        return remote(own[b].at[rows_of(peer)], part_in[b].at[sub],
                      part_send.at[b], part_recv.at[b], dom, peer)

    def part_all(b):
        return bulk(part_in[b].at[0 : n_sub - 1], part_send.at[b], part_recv.at[b])

    def z_copy(b, peer):
        return remote(z_in[b].at[col], z_in[b].at[col],
                      z_send.at[b], z_recv.at[b], row * N_Z + peer, sub)

    def z_all(b):
        return bulk(z_in[b].at[0 : N_Z - 1], z_send.at[b], z_recv.at[b])

    def y_copy(b, peer):
        return remote(y_in[b].at[row], y_in[b].at[row],
                      y_send.at[b], y_recv.at[b], peer * N_Z + col, sub)

    def y_all(b):
        return bulk(y_in[b].at[0 : n_y - 1], y_send.at[b], y_recv.at[b])

    def out_copy(b, peer):
        return remote(sums[b].at[rows_of(sub)], sums[b].at[rows_of(sub)],
                      out_send.at[b], out_recv.at[b], dom, peer)

    def out_all(b):
        return bulk(sums[b].at[0 : (n_sub - 1) * share], out_send.at[b], out_recv.at[b])

    def total(ref, count):
        result = ref[0]
        for k in range(1, count):
            result = result + ref[k]
        return result

    def sum_begin(b):
        for k in far_first(n_sub):
            part_copy(b, sub_peer(k)).start()
        part_in[b][sub] = own[b][rows_of(sub), :]

    def sum_along_z(b):
        part_all(b).wait_recv()
        z_in[b][col] = total(part_in[b], n_sub)
        for k in far_first(N_Z):
            z_copy(b, z_peer(k)).start()

    def sum_along_y(b):
        z_all(b).wait_recv()
        y_in[b][row] = total(z_in[b], N_Z)
        for k in far_first(n_y):
            y_copy(b, y_peer(k)).start()

    def sum_back(b):
        y_all(b).wait_recv()
        sums[b][rows_of(sub), :] = total(y_in[b], n_y)
        for k in far_first(n_sub):
            out_copy(b, sub_peer(k)).start()

    def sum_end(b):
        out_all(b).wait_recv()

    def sum_sent(b):
        for copies in (part_all, z_all, y_all, out_all):
            copies(b).wait_send()

    def rs_sent(j):
        rs_all(j).wait_send()

    def ag_sent(j):
        for area in range(3):
            ag_all(j, area).wait_send()

    root_ref[...] = lax.rsqrt(jnp.sum(weight_ref[...], axis=0, keepdims=True))

    def place(i, carry):
        base = pl.multiple_of(i * BUILD_ROWS, BUILD_ROWS)
        ids = base + lax.broadcasted_iota(jnp.int32, (BUILD_ROWS, nodes), 0)
        place_ref[pl.ds(base, BUILD_ROWS), :] = jnp.where(
            ids == slot_ref[...], 1.0, 0.0
        ).astype(jnp.bfloat16)
        return carry

    lax.fori_loop(0, slots // BUILD_ROWS, place, 0)

    def build(i, carry):
        base = pl.multiple_of(i * BUILD_ROWS, BUILD_ROWS)
        ids = base + lax.broadcasted_iota(jnp.int32, (BUILD_ROWS, nodes), 0)
        summed = jnp.zeros((BUILD_ROWS, nodes), jnp.float32)
        for k in range(links_ref.shape[0]):
            summed = summed + jnp.where(
                ids == links_ref[k : k + 1, :], weight_ref[k : k + 1, :], 0.0
            )
        high, low = split(summed * root_ref[...])
        table_hi[pl.ds(base, BUILD_ROWS), :] = high
        table_lo[pl.ds(base, BUILD_ROWS), :] = low
        return carry

    def contribute(j, vectors):
        high, low = split(root_ref[...] * vectors)
        spread = lax.dot_general(
            jnp.concatenate([high, low], axis=0),
            place_ref[...],
            (((1,), (1,)), ((), ())),
            preferred_element_type=jnp.float32,
        )
        contrib[j] = (spread[:block] + spread[block:]).reshape(n_sub, share, slots)
        return high, low

    def apply(high, low, first, count):
        upper = jnp.dot(
            jnp.concatenate([high, low], axis=0),
            table_hi[first : first + count, :],
            preferred_element_type=jnp.float32,
        )
        lower = jnp.dot(
            high, table_lo[first : first + count, :], preferred_element_type=jnp.float32
        )
        return upper[:block] + upper[block:] + lower

    def affinity(j, vectors, while_reduced, while_gathered):
        high, low = contribute(j, vectors)
        if j == 0:
            pl.semaphore_wait(barrier, 3 * n_sub - 1 + N_Z - 1 + n_y - 1)
        for k in far_first(n_sub):
            rs_copy(j, sub_peer(k)).start()
        gathered[j, sub] = contrib[j, sub]
        while_reduced()
        summed = apply(high, low, 0, nodes)
        rs_all(j).wait_recv()
        pools[j, 1, sub] = total(gathered.at[j], n_sub)
        for k in far_first(n_sub) + [0]:
            ag_copy(j, 0, sub_peer(k), 2).start()
            ag_copy(j, 2, sub_peer(k), 0).start()
        for k in far_first(n_sub):
            ag_copy(j, 1, sub_peer(k), 1).start()
        while_gathered()
        for area in (1, 0, 2):
            ag_all(j, area).wait_recv()
            high, low = split(pools[j, area].reshape(block, slots))
            summed = summed + apply(high, low, nodes + area * slots, slots)
        return summed

    def build_table():
        lax.fori_loop(0, table_hi.shape[0] // BUILD_ROWS, build, 0)

    def moments_first():
        own_a[:, 0:block] = nt(start_ref[...], start_ref[...])
        own_a[:, 3 * block :] = jnp.zeros((block, block), jnp.float32)
        own_c[:, block:] = jnp.zeros((block, block), jnp.float32)
        rs_sent(0)

    def moments_second():
        own_a[:, block : 2 * block] = nt(start_ref[...], one_ref[...])
        own_a[:, 2 * block : 3 * block] = nt(one_ref[...], one_ref[...])
        sum_begin(0)
        ag_sent(0)

    def second_gathered():
        sum_along_z(0)
        rs_sent(1)

    def third_reduced():
        sum_along_y(0)
        ag_sent(1)
        sum_along_z(1)

    def third_gathered():
        sum_back(0)
        rs_sent(2)
        sum_along_y(1)

    one_ref[...] = affinity(0, start_ref[...], build_table, moments_first)
    two_ref[...] = affinity(1, one_ref[...], moments_second, second_gathered)
    own_b[:, 0:block] = nt(one_ref[...], two_ref[...])
    own_b[:, block:] = nt(two_ref[...], two_ref[...])
    sum_begin(1)
    three = affinity(2, two_ref[...], third_reduced, third_gathered)
    own_c[:, 0:block] = nt(two_ref[...], three)

    def moment(b, c):
        return mean_with_transpose(sums[b][:, c * block : (c + 1) * block] * scale)

    sum_begin(2)
    sum_end(0)
    m0, m1, m2 = moment(0, 0), moment(0, 1), moment(0, 2)
    upper, first, below, rest = factor_one(m0, m1, m2)
    sum_back(1)
    sum_along_z(2)
    inverse = inverse_one(first, below, rest)
    sum_end(1)
    m3, m4 = moment(1, 0), moment(1, 1)
    tilted, gram = filter_one(inverse, upper, m1, m2, m3)
    sum_along_y(2)
    powers = jnp.concatenate([start_ref[...], one_ref[...], two_ref[...]], axis=0)
    tail, products, mixed, rotated = ritz_one(inverse, tilted, gram, [m0, m1, m2, m3, m4], powers)
    along, left = residual_and_search(products)
    sum_back(2)
    normal, overlap, rest, shared, theta = eliminate_search(along, left)
    last, partial, rotated = basis_two(normal, overlap, rest, shared, theta, mixed, rotated)
    tail_ref[...] = nt(tail, last)
    partial_ref[...] = partial
    rotated_ref[...] = rotated
    ag_sent(2)
    for b in range(len(WIDTHS)):
        sum_sent(b)
    sum_end(2)


def per_device(start, links, link_weight, pool_slot):
    n_dom = lax.axis_size("dom")
    n_sub = lax.axis_size("sub")
    n_y = n_dom // N_Z
    block, nodes = start.shape
    slots = SLOT_DEV * n_sub
    share = block // n_sub
    entries = nodes + 3 * slots
    f32 = jnp.float32
    vmem = pl.BlockSpec(memory_space=VMEM)
    limit = 32 * 1024 * 1024

    def array(*shape):
        return jax.ShapeDtypeStruct(shape, f32)

    def buffers(*shape):
        return [VMEM(shape + (width,), f32) for width in WIDTHS]

    tail, partial, rotated, last = pl.pallas_call(
        functools.partial(sums_kernel, n_dom, n_sub),
        out_shape=(
            array(block, block),
            array(3 * block, 3 * block),
            array(3 * block, nodes),
            array(block, WIDTHS[2]),
        ),
        in_specs=[vmem] * 4,
        out_specs=(vmem,) * 4,
        scratch_shapes=[
            VMEM((block, nodes), f32),
            VMEM((block, nodes), f32),
            VMEM((1, nodes), f32),
            VMEM((slots, nodes), jnp.bfloat16),
            VMEM((entries, nodes), jnp.bfloat16),
            VMEM((entries, nodes), jnp.bfloat16),
            VMEM((ROUNDS, n_sub, share, slots), f32),
            VMEM((ROUNDS, n_sub, share, slots), f32),
            VMEM((ROUNDS, 3, n_sub, share, slots), f32),
            *buffers(block),
            *buffers(n_sub, share),
            *buffers(N_Z, share),
            *buffers(n_y, share),
            *buffers(block)[:2],
            DMA((ROUNDS,)),
            DMA((ROUNDS,)),
            DMA((ROUNDS, 3)),
            DMA((ROUNDS, 3)),
            *[DMA((len(WIDTHS),)) for _ in range(8)],
        ],
        compiler_params=pltpu.CompilerParams(
            collective_id=0, has_side_effects=True, vmem_limit_bytes=limit
        ),
        name="powers_and_sums",
    )(start, links, link_weight, pool_slot.reshape(1, nodes))
    return pl.pallas_call(
        functools.partial(ritz_kernel, 1.0 / (nodes * n_dom * n_sub)),
        out_shape=(array(block, nodes), array(block, block)),
        in_specs=[vmem] * 4,
        out_specs=(vmem,) * 2,
        compiler_params=pltpu.CompilerParams(vmem_limit_bytes=limit),
        name="ritz_steps",
    )(last, tail, partial, rotated)


def solution(mesh):
    placed = (
        P(None, ("dom", "sub")),
        P(None, ("dom", "sub")),
        P(None, ("dom", "sub")),
        P(("dom", "sub")),
    )
    return jax.shard_map(
        per_device,
        mesh=mesh,
        in_specs=placed,
        out_specs=(P(None, ("dom", "sub")), P()),
        check_vma=False,
    )
```

```python
import functools

import jax
import jax.numpy as jnp
from jax import lax
from jax.experimental import pallas as pl
from jax.experimental.pallas import tpu as pltpu
from jax.sharding import PartitionSpec as P

MESH = pl.DeviceIdType.MESH
VMEM = pltpu.VMEM
DMA = pltpu.SemaphoreType.DMA
SLOT_DEV = 64
ROUNDS = 3
BUILD_ROWS = 64
N_Z = 12
SUBLANES = 8
LANES = 128
WIDTHS = (2 * LANES, LANES, LANES)


def split(values):
    high = values.astype(jnp.bfloat16)
    low = (values - high.astype(jnp.float32)).astype(jnp.bfloat16)
    return high, low


def product(left, right, dims):
    return lax.dot_general(
        left, right, (dims, ((), ())),
        precision=lax.Precision.HIGHEST, preferred_element_type=jnp.float32,
    )


def nn(left, right):
    return product(left, right, ((1,), (0,)))


def nt(left, right):
    return product(left, right, ((1,), (1,)))


def tn(left, right):
    return product(left, right, ((0,), (0,)))


def eye(size):
    rows = lax.broadcasted_iota(jnp.int32, (size, size), 0)
    cols = lax.broadcasted_iota(jnp.int32, (size, size), 1)
    return jnp.where(rows == cols, 1.0, 0.0)


def mean_with_transpose(matrix):
    return 0.5 * (matrix + matrix.T)


def cholesky_and_inverse(matrix):
    size = matrix.shape[0]
    width = 2 * size
    rows = jnp.concatenate([matrix, eye(size)], axis=1)
    ids = lax.broadcasted_iota(jnp.int32, (size, width), 0)
    done = []
    for first in range(0, size, SUBLANES):
        left = size - first
        tile = (SUBLANES, width)
        spread = [
            jnp.broadcast_to(rows[:, first + k : first + k + 1], (left, width))
            for k in range(SUBLANES)
        ]
        for k in range(SUBLANES):
            inverse = 1.0 / jnp.broadcast_to(spread[k][k : k + 1, :], tile)
            factor = jnp.where(ids[:left] > k, spread[k], 0.0)

            def eliminate(values):
                pivot_row = jnp.broadcast_to(values[k : k + 1, :], tile) * inverse
                return values - factor * jnp.concatenate([pivot_row] * (left // SUBLANES), axis=0)

            rows = eliminate(rows)
            for c in range(k + 1, SUBLANES):
                spread[c] = eliminate(spread[c])
        pivot = spread[0][:SUBLANES]
        for k in range(1, SUBLANES):
            pivot = jnp.where(ids[:SUBLANES] == k, spread[k][:SUBLANES], pivot)
        done.append(rows[:SUBLANES] * lax.rsqrt(pivot))
        rows = rows[SUBLANES:]
    result = jnp.concatenate(done, axis=0)
    upper = result[:, :size]
    row_ids = lax.broadcasted_iota(jnp.int32, (size, size), 0)
    col_ids = lax.broadcasted_iota(jnp.int32, (size, size), 1)
    return jnp.where(col_ids >= row_ids, upper, 0.0), result[:, size:]


def blocks(rows):
    return jnp.concatenate([jnp.concatenate(row, axis=1) for row in rows], axis=0)


def filtered(reduced, first):
    half = 0.5 * (reduced + eye(reduced.shape[0]))
    square = nn(half, half)
    return nn(square, first(square))


def factor_one(m0, m1, m2):
    upper, first = cholesky_and_inverse(m0)
    below = nt(m1, first)
    return upper, first, below, m2 - nt(below, below)


def inverse_one(first, below, rest):
    _, second = cholesky_and_inverse(rest)
    corner = -nn(second, nn(below, first))
    return blocks([[first, jnp.zeros_like(first)], [corner, second]])


def filter_one(inverse, upper, m1, m2, m3):
    block = upper.shape[0]
    reduced = nt(nn(inverse, blocks([[m1, m2], [m2, m3]])), inverse)
    tilted = filtered(reduced, lambda square: nn(square[:, :block], upper))
    return tilted, tn(tilted, tilted)


def hankel(moments):
    return blocks([moments[i : i + 3] for i in range(3)])


def diagonal(part, count):
    zero = jnp.zeros_like(part)
    return blocks([[part if i == j else zero for j in range(count)] for i in range(count)])


def ritz_one(inverse, tilted, gram, moments, powers):
    block = gram.shape[0]
    coeffs = tn(inverse, tilted)
    head, tail = coeffs[:block], coeffs[block:]
    zero = jnp.zeros_like(head)
    spanned = blocks([[zero, zero, head], [tail, head, tail], [zero, tail, zero]])
    _, normal = cholesky_and_inverse(gram)
    products = tn(spanned, nn(hankel(moments), spanned[:, : 2 * block]))
    mixed = tn(spanned, nn(hankel(moments[1:] + [zero]), spanned))
    rotated = tn(spanned, powers)
    thrice = diagonal(normal, 3)
    return (
        nt(tail, normal),
        nt(nn(thrice, products), diagonal(normal, 2)),
        nt(nn(thrice, mixed), thrice),
        nn(thrice, rotated),
    )


def residual_and_search(products):
    block = products.shape[1] // 2
    along = products[2 * block :]
    return along, products[: 2 * block] - tn(along, along)


def eliminate_search(along, left):
    block = along.shape[0]
    shared, theta = along[:, :block], along[:, block:]
    _, normal = cholesky_and_inverse(left[:block, :block])
    overlap = nn(normal, left[:block, block:])
    return normal, overlap, left[block:, block:] - tn(overlap, overlap), shared, theta


def basis_two(normal, overlap, rest, shared, theta, mixed, rotated):
    block = rest.shape[0]
    zero = jnp.zeros_like(rest)
    _, last = cholesky_and_inverse(rest)
    search = normal.T
    along = nn(shared, search)
    turn = blocks(
        [
            [zero, search, -nn(search, overlap)],
            [zero, zero, eye(block)],
            [eye(block), -along, nn(along, overlap) - theta],
        ]
    )
    mixed = tn(turn, nn(mixed, turn))
    rotated = tn(turn, rotated)
    above, below = mixed[: 2 * block], nn(last, mixed[2 * block :])
    reduced = blocks(
        [
            [above[:, : 2 * block], nt(above[:, 2 * block :], last)],
            [below[:, : 2 * block], nt(below[:, 2 * block :], last)],
        ]
    )
    rotated = jnp.concatenate([rotated[: 2 * block], nn(last, rotated[2 * block :])], axis=0)
    return last, reduced, rotated


def ritz_kernel(scale, sums_ref, tail_ref, partial_ref, rotated_ref, eigen_ref, ritz_ref):
    block = ritz_ref.shape[0]
    last = mean_with_transpose(sums_ref[:, :block] * scale)
    tail = tail_ref[...]
    zero = jnp.zeros((block, block), jnp.float32)
    corner = tn(tail, nn(last, tail))
    reduced = partial_ref[...] + blocks(
        [[zero, zero, zero], [zero, zero, zero], [zero, zero, corner]]
    )
    tilted = filtered(reduced, lambda square: square[:, :block])
    _, normal = cholesky_and_inverse(tn(tilted, tilted))
    turned = tn(tilted, rotated_ref[...])
    projected = tn(tilted, nn(reduced, tilted))
    eigen_ref[...] = nn(normal, turned)
    ritz_ref[...] = nt(nn(normal, projected), normal)


def far_first(count):
    return sorted(range(1, count), key=lambda k: -min(k, count - k))


def sums_kernel(
    n_dom,
    n_sub,
    start_ref,
    links_ref,
    weight_ref,
    slot_ref,
    tail_ref,
    partial_ref,
    rotated_ref,
    last_ref,
    one_ref,
    two_ref,
    root_ref,
    place_ref,
    table_hi,
    table_lo,
    contrib,
    gathered,
    pools,
    own_a,
    own_b,
    own_c,
    part_a,
    part_b,
    part_c,
    z_a,
    z_b,
    z_c,
    y_a,
    y_b,
    y_c,
    sums_a,
    sums_b,
    rs_send,
    rs_recv,
    ag_send,
    ag_recv,
    part_send,
    part_recv,
    z_send,
    z_recv,
    y_send,
    y_recv,
    out_send,
    out_recv,
):
    dom = lax.axis_index("dom")
    sub = lax.axis_index("sub")
    n_y = n_dom // N_Z
    row = lax.div(dom, N_Z)
    col = lax.rem(dom, N_Z)
    block = start_ref.shape[0]
    nodes = start_ref.shape[1]
    slots = place_ref.shape[0]
    share = block // n_sub
    scale = 1.0 / (nodes * n_dom * n_sub)
    own = (own_a, own_b, own_c)
    part_in = (part_a, part_b, part_c)
    z_in = (z_a, z_b, z_c)
    y_in = (y_a, y_b, y_c)
    sums = (sums_a, sums_b, last_ref)

    def sub_peer(k):
        return lax.rem(sub + k, n_sub)

    def dom_peer(area):
        return lax.rem(dom + (area + n_dom - 1), n_dom)

    def z_peer(k):
        return lax.rem(col + k, N_Z)

    def y_peer(k):
        return lax.rem(row + k, n_y)

    def remote(src, dst, send, recv, d, s):
        return pltpu.make_async_remote_copy(
            src_ref=src, dst_ref=dst, send_sem=send, recv_sem=recv,
            device_id=(d, s), device_id_type=MESH,
        )

    barrier = pltpu.get_barrier_semaphore()

    def greet(d, s):
        pl.semaphore_signal(barrier, inc=1, device_id=(d, s), device_id_type=MESH)

    for k in far_first(N_Z):
        greet(row * N_Z + z_peer(k), sub)
    for k in far_first(n_y):
        greet(y_peer(k) * N_Z + col, sub)
    for k in far_first(n_sub) + [0]:
        greet(dom_peer(0), sub_peer(k))
        greet(dom_peer(2), sub_peer(k))
    for k in far_first(n_sub):
        greet(dom, sub_peer(k))

    def bulk(ref, send, recv):
        return remote(ref, ref, send, recv, dom, sub_peer(1))

    def rs_copy(j, peer):
        return remote(contrib.at[j, peer], gathered.at[j, sub],
                      rs_send.at[j], rs_recv.at[j], dom, peer)

    def rs_all(j):
        return bulk(gathered.at[j, 0 : n_sub - 1], rs_send.at[j], rs_recv.at[j])

    def ag_copy(j, to, peer, area):
        return remote(pools.at[j, 1, sub], pools.at[j, area, sub],
                      ag_send.at[j, to], ag_recv.at[j, area], dom_peer(to), peer)

    def ag_all(j, area):
        some = pools.at[j, area, 0 : n_sub - 1] if area == 1 else pools.at[j, area]
        return bulk(some, ag_send.at[j, area], ag_recv.at[j, area])

    def rows_of(p):
        return pl.ds(pl.multiple_of(p * share, share), share)

    def part_copy(b, peer):
        return remote(own[b].at[rows_of(peer)], part_in[b].at[sub],
                      part_send.at[b], part_recv.at[b], dom, peer)

    def part_all(b):
        return bulk(part_in[b].at[0 : n_sub - 1], part_send.at[b], part_recv.at[b])

    def z_copy(b, peer):
        return remote(z_in[b].at[col], z_in[b].at[col],
                      z_send.at[b], z_recv.at[b], row * N_Z + peer, sub)

    def z_all(b):
        return bulk(z_in[b].at[0 : N_Z - 1], z_send.at[b], z_recv.at[b])

    def y_copy(b, peer):
        return remote(y_in[b].at[row], y_in[b].at[row],
                      y_send.at[b], y_recv.at[b], peer * N_Z + col, sub)

    def y_all(b):
        return bulk(y_in[b].at[0 : n_y - 1], y_send.at[b], y_recv.at[b])

    def out_copy(b, peer):
        return remote(sums[b].at[rows_of(sub)], sums[b].at[rows_of(sub)],
                      out_send.at[b], out_recv.at[b], dom, peer)

    def out_all(b):
        return bulk(sums[b].at[0 : (n_sub - 1) * share], out_send.at[b], out_recv.at[b])

    def total(ref, count):
        result = ref[0]
        for k in range(1, count):
            result = result + ref[k]
        return result

    def sum_begin(b):
        for k in far_first(n_sub):
            part_copy(b, sub_peer(k)).start()
        part_in[b][sub] = own[b][rows_of(sub), :]

    def sum_along_z(b):
        part_all(b).wait_recv()
        z_in[b][col] = total(part_in[b], n_sub)
        for k in far_first(N_Z):
            z_copy(b, z_peer(k)).start()

    def sum_along_y(b):
        z_all(b).wait_recv()
        y_in[b][row] = total(z_in[b], N_Z)
        for k in far_first(n_y):
            y_copy(b, y_peer(k)).start()

    def sum_back(b):
        y_all(b).wait_recv()
        sums[b][rows_of(sub), :] = total(y_in[b], n_y)
        for k in far_first(n_sub):
            out_copy(b, sub_peer(k)).start()

    def sum_end(b):
        out_all(b).wait_recv()

    def sum_sent(b):
        for copies in (part_all, z_all, y_all, out_all):
            copies(b).wait_send()

    def rs_sent(j):
        rs_all(j).wait_send()

    def ag_sent(j):
        for area in range(3):
            ag_all(j, area).wait_send()

    root_ref[...] = lax.rsqrt(jnp.sum(weight_ref[...], axis=0, keepdims=True))

    def place(i, carry):
        base = pl.multiple_of(i * BUILD_ROWS, BUILD_ROWS)
        ids = base + lax.broadcasted_iota(jnp.int32, (BUILD_ROWS, nodes), 0)
        place_ref[pl.ds(base, BUILD_ROWS), :] = jnp.where(
            ids == slot_ref[...], 1.0, 0.0
        ).astype(jnp.bfloat16)
        return carry

    lax.fori_loop(0, slots // BUILD_ROWS, place, 0)

    def build(i, carry):
        base = pl.multiple_of(i * BUILD_ROWS, BUILD_ROWS)
        ids = base + lax.broadcasted_iota(jnp.int32, (BUILD_ROWS, nodes), 0)
        summed = jnp.zeros((BUILD_ROWS, nodes), jnp.float32)
        for k in range(links_ref.shape[0]):
            summed = summed + jnp.where(
                ids == links_ref[k : k + 1, :], weight_ref[k : k + 1, :], 0.0
            )
        high, low = split(summed * root_ref[...])
        table_hi[pl.ds(base, BUILD_ROWS), :] = high
        table_lo[pl.ds(base, BUILD_ROWS), :] = low
        return carry

    def contribute(j, vectors):
        high, low = split(root_ref[...] * vectors)
        spread = lax.dot_general(
            jnp.concatenate([high, low], axis=0),
            place_ref[...],
            (((1,), (1,)), ((), ())),
            preferred_element_type=jnp.float32,
        )
        contrib[j] = (spread[:block] + spread[block:]).reshape(n_sub, share, slots)
        return high, low

    def apply(high, low, first, count):
        upper = jnp.dot(
            jnp.concatenate([high, low], axis=0),
            table_hi[first : first + count, :],
            preferred_element_type=jnp.float32,
        )
        lower = jnp.dot(
            high, table_lo[first : first + count, :], preferred_element_type=jnp.float32
        )
        return upper[:block] + upper[block:] + lower

    def affinity(j, vectors, while_reduced, while_gathered):
        high, low = contribute(j, vectors)
        if j == 0:
            pl.semaphore_wait(barrier, 3 * n_sub - 1 + N_Z - 1 + n_y - 1)
        for k in far_first(n_sub):
            rs_copy(j, sub_peer(k)).start()
        gathered[j, sub] = contrib[j, sub]
        while_reduced()
        summed = apply(high, low, 0, nodes)
        rs_all(j).wait_recv()
        pools[j, 1, sub] = total(gathered.at[j], n_sub)
        for k in far_first(n_sub) + [0]:
            ag_copy(j, 0, sub_peer(k), 2).start()
            ag_copy(j, 2, sub_peer(k), 0).start()
        for k in far_first(n_sub):
            ag_copy(j, 1, sub_peer(k), 1).start()
        while_gathered()
        for area in (1, 0, 2):
            ag_all(j, area).wait_recv()
            high, low = split(pools[j, area].reshape(block, slots))
            summed = summed + apply(high, low, nodes + area * slots, slots)
        return summed

    parts = table_hi.shape[0] // BUILD_ROWS
    early = (nodes + slots) // BUILD_ROWS

    def build_table():
        lax.fori_loop(0, early, build, 0)

    def moments_first():
        lax.fori_loop(early, parts, build, 0)
        own_a[:, 0:block] = nt(start_ref[...], start_ref[...])
        own_a[:, 3 * block :] = jnp.zeros((block, block), jnp.float32)
        own_c[:, block:] = jnp.zeros((block, block), jnp.float32)
        rs_sent(0)

    def moments_second():
        own_a[:, block : 2 * block] = nt(start_ref[...], one_ref[...])
        own_a[:, 2 * block : 3 * block] = nt(one_ref[...], one_ref[...])
        sum_begin(0)
        ag_sent(0)

    def second_gathered():
        sum_along_z(0)
        rs_sent(1)

    def third_reduced():
        sum_along_y(0)
        ag_sent(1)
        sum_along_z(1)

    def third_gathered():
        sum_back(0)
        rs_sent(2)
        sum_along_y(1)

    one_ref[...] = affinity(0, start_ref[...], build_table, moments_first)
    two_ref[...] = affinity(1, one_ref[...], moments_second, second_gathered)
    own_b[:, 0:block] = nt(one_ref[...], two_ref[...])
    own_b[:, block:] = nt(two_ref[...], two_ref[...])
    sum_begin(1)
    three = affinity(2, two_ref[...], third_reduced, third_gathered)
    own_c[:, 0:block] = nt(two_ref[...], three)

    def moment(b, c):
        return mean_with_transpose(sums[b][:, c * block : (c + 1) * block] * scale)

    sum_begin(2)
    sum_end(0)
    m0, m1, m2 = moment(0, 0), moment(0, 1), moment(0, 2)
    upper, first, below, rest = factor_one(m0, m1, m2)
    sum_back(1)
    sum_along_z(2)
    inverse = inverse_one(first, below, rest)
    sum_end(1)
    m3, m4 = moment(1, 0), moment(1, 1)
    tilted, gram = filter_one(inverse, upper, m1, m2, m3)
    sum_along_y(2)
    powers = jnp.concatenate([start_ref[...], one_ref[...], two_ref[...]], axis=0)
    tail, products, mixed, rotated = ritz_one(inverse, tilted, gram, [m0, m1, m2, m3, m4], powers)
    along, left = residual_and_search(products)
    sum_back(2)
    normal, overlap, rest, shared, theta = eliminate_search(along, left)
    last, partial, rotated = basis_two(normal, overlap, rest, shared, theta, mixed, rotated)
    tail_ref[...] = nt(tail, last)
    partial_ref[...] = partial
    rotated_ref[...] = rotated
    ag_sent(2)
    for b in range(len(WIDTHS)):
        sum_sent(b)
    sum_end(2)


def per_device(start, links, link_weight, pool_slot):
    n_dom = lax.axis_size("dom")
    n_sub = lax.axis_size("sub")
    n_y = n_dom // N_Z
    block, nodes = start.shape
    slots = SLOT_DEV * n_sub
    share = block // n_sub
    entries = nodes + 3 * slots
    f32 = jnp.float32
    vmem = pl.BlockSpec(memory_space=VMEM)
    limit = 32 * 1024 * 1024

    def array(*shape):
        return jax.ShapeDtypeStruct(shape, f32)

    def buffers(*shape):
        return [VMEM(shape + (width,), f32) for width in WIDTHS]

    tail, partial, rotated, last = pl.pallas_call(
        functools.partial(sums_kernel, n_dom, n_sub),
        out_shape=(
            array(block, block),
            array(3 * block, 3 * block),
            array(3 * block, nodes),
            array(block, WIDTHS[2]),
        ),
        in_specs=[vmem] * 4,
        out_specs=(vmem,) * 4,
        scratch_shapes=[
            VMEM((block, nodes), f32),
            VMEM((block, nodes), f32),
            VMEM((1, nodes), f32),
            VMEM((slots, nodes), jnp.bfloat16),
            VMEM((entries, nodes), jnp.bfloat16),
            VMEM((entries, nodes), jnp.bfloat16),
            VMEM((ROUNDS, n_sub, share, slots), f32),
            VMEM((ROUNDS, n_sub, share, slots), f32),
            VMEM((ROUNDS, 3, n_sub, share, slots), f32),
            *buffers(block),
            *buffers(n_sub, share),
            *buffers(N_Z, share),
            *buffers(n_y, share),
            *buffers(block)[:2],
            DMA((ROUNDS,)),
            DMA((ROUNDS,)),
            DMA((ROUNDS, 3)),
            DMA((ROUNDS, 3)),
            *[DMA((len(WIDTHS),)) for _ in range(8)],
        ],
        compiler_params=pltpu.CompilerParams(
            collective_id=0, has_side_effects=True, vmem_limit_bytes=limit
        ),
        name="powers_and_sums",
    )(start, links, link_weight, pool_slot.reshape(1, nodes))
    return pl.pallas_call(
        functools.partial(ritz_kernel, 1.0 / (nodes * n_dom * n_sub)),
        out_shape=(array(block, nodes), array(block, block)),
        in_specs=[vmem] * 4,
        out_specs=(vmem,) * 2,
        compiler_params=pltpu.CompilerParams(vmem_limit_bytes=limit),
        name="ritz_steps",
    )(last, tail, partial, rotated)


def solution(mesh):
    placed = (
        P(None, ("dom", "sub")),
        P(None, ("dom", "sub")),
        P(None, ("dom", "sub")),
        P(("dom", "sub")),
    )
    return jax.shard_map(
        per_device,
        mesh=mesh,
        in_specs=placed,
        out_specs=(P(None, ("dom", "sub")), P()),
        check_vma=False,
    )
```
